128 devices in a mesh: face: 16 (over x, z), rep: 8 (over y, core).
Axes of the slice: x: 4, y: 4, z: 4, core: 2. Of those that a mesh axis runs over, the one named last changes fastest.
Arguments:
- fields: bfloat16 [8, 32, 32, 32, 256], P('rep', 'face'), may hold values from -6 to 6
- out_grad: bfloat16 [8, 32, 32, 32, 256], P('rep', 'face'), may hold values from -6 to 6
- kernel: bfloat16 [7, 7, 256], replicated, may hold values from -0.875 to 0.875
- ln_gain: float32 [256], replicated, may hold values from 0.1 to 1.9
- ln_shift: float32 [256], replicated, may hold values from -3 to 3
- w_in: bfloat16 [256, 1024], replicated, may hold values from -0.375 to 0.375
- w_out: bfloat16 [1024, 256], replicated, may hold values from -0.1875 to 0.1875
- edge_tile: int32 [32, 4], replicated, may hold values from 0 to 31, as said below
- edge_code: int32 [32, 4], replicated, may hold values from 0 to 7, as said below
- corner_tile: int32 [32, 4], replicated, may hold values from 0 to 31, as said below
- corner_code: int32 [32, 4], replicated, may hold values from 0 to 7, as said below
Outputs:
- result: bfloat16 [8, 32, 32, 32, 256], P('rep', 'face')
- grad_input: bfloat16 [8, 32, 32, 32, 256], P('rep', 'face')
- grad_kernel: float32 [7, 7, 256], replicated
- grad_gain: float32 [256], replicated
- grad_shift: float32 [256], replicated
- grad_win: float32 [256, 1024], replicated
- grad_wout: float32 [1024, 256], replicated
The draws below stay inside these ranges and needn't reach their ends.
Inputs may be any that keep to these rules, and one draw needn't show every extreme that they name: `edge_tile`: the tiles form 32/4 faces of 4 slabs each, numbered face-major (tile = 4 face + slab). The north and south neighbours of a slab inside a face are the slabs beside it in the same face. The first slab's north neighbour is the last slab of the face given by a permutation of faces. Every slab's east neighbour is the same slab of the face given by a second permutation, and its west neighbour is given by the inverse. Which faces are paired is redrawn with the seed. `edge_code`: code % 4 names the neighbour's edge and is (e + 2) % 4 for edge e. code // 4 is 1 where the direction along the edge is reversed, which happens only across face seams and is the same from both sides of a seam. `corner_tile`: the top-left and top-right corners are owned by the north neighbour of the west and east neighbours; the bottom-right and bottom-left corners by their south neighbours. `corner_code`: code % 4 names the owner's corner and is (k + 2) % 4 for corner k. code // 4 is 1 where the block is transposed, which happens only where the corner lies across an east or west face seam that reverses.
All inputs are finite; a program needn't handle non-finite values.
Results may differ from the reference program's by a relative error of at most 0.0056.
Values may be sent and summed in bfloat16 or wider, within the bound.
No kernel may reach another device: no remote copies, remote signals or barrier semaphores. Data moves between devices by JAX's collectives and lax.ppermute only.
A program may use at most 128 MiB of HBM per device.

```python
import math
import jax
import jax.numpy as jnp
from jax import lax

C = 256
HID = 1024
P_SIZE = 32
TILES = 32
REPS = 8


def halo_tables(key):
    faces = TILES // 4
    keys = jax.random.split(key, 4)
    face_ids = jnp.arange(faces, dtype=jnp.int32)
    upward = jax.random.permutation(keys[0], faces).astype(jnp.int32)
    sideways = jax.random.permutation(keys[1], faces).astype(jnp.int32)
    upward_inv = jnp.zeros((faces,), jnp.int32).at[upward].set(face_ids)
    sideways_inv = jnp.zeros((faces,), jnp.int32).at[sideways].set(face_ids)
    flip_up = jax.random.randint(keys[2], (faces,), 0, 2, dtype=jnp.int32)
    flip_side = jax.random.randint(keys[3], (faces,), 0, 2, dtype=jnp.int32)
    flip_side = flip_side.at[0].set(1).at[1].set(0)
    tiles = jnp.arange(TILES, dtype=jnp.int32)
    face_of = tiles // 4
    slab = tiles % 4
    north = jnp.where(slab > 0, tiles - 1, upward[face_of] * 4 + 3)
    north_code = jnp.where(slab > 0, 2, 2 + 4 * flip_up[face_of])
    south = jnp.where(slab < 3, tiles + 1, upward_inv[face_of] * 4)
    south_code = jnp.where(slab < 3, 0, 4 * flip_up[upward_inv[face_of]])
    east = sideways[face_of] * 4 + slab
    west = sideways_inv[face_of] * 4 + slab
    flip_east = flip_side[face_of]
    flip_west = flip_side[sideways_inv[face_of]]
    edge_tile = jnp.stack([north, east, south, west], axis=1).astype(jnp.int32)
    edge_code = jnp.stack([north_code, 3 + 4 * flip_east, south_code, 1 + 4 * flip_west], axis=1).astype(jnp.int32)
    corner_tile = jnp.stack([north[west], north[east], south[east], south[west]], axis=1).astype(jnp.int32)
    corner_code = jnp.stack([2 + 4 * flip_west, 3 + 4 * flip_east, 4 * flip_east, 1 + 4 * flip_west], axis=1).astype(jnp.int32)
    return (edge_tile, edge_code, corner_tile, corner_code)


def draw_edge_tile(key, part):
    return halo_tables(key)[0]


def draw_edge_code(key, part):
    return halo_tables(key)[1]


def draw_corner_tile(key, part):
    return halo_tables(key)[2]


def draw_corner_code(key, part):
    return halo_tables(key)[3]


def level_of(key, shape, cuts, least, largest):
    loudness, own = 1.0, jax.random.fold_in(key, 6)
    for axis_at, parts in cuts:
        heights = jnp.exp(jax.random.uniform(jax.random.fold_in(own, axis_at), (parts,), jnp.float32, least / len(cuts), largest / len(cuts)))
        loudness = loudness * jnp.repeat(heights, shape[axis_at] // parts).reshape([-1 if axis == axis_at else 1 for axis in range(len(shape))])
    return loudness


def centred(own_key, shape, deviation, bound, shards=(), kind=jnp.bfloat16):
    loudness = level_of(own_key, shape, shards, -0.22, 0.18) if shards else 1.0
    result = jax.random.normal(own_key, shape, jnp.float32) * deviation * loudness
    return jnp.minimum(jnp.maximum(result, -bound), bound).astype(kind)


def setup_inputs(seed: int = 0) -> dict:
    splits = jax.random.split(jax.random.key(seed), 12)
    fields = centred(splits[0], (REPS, TILES, P_SIZE, P_SIZE, C), 1.0, 6.0, ((0, 8), (1, 16)))
    out_grad = centred(splits[1], (REPS, TILES, P_SIZE, P_SIZE, C), 1.0, 6.0, ((0, 8), (1, 16)))
    kernel = centred(splits[2], (7, 7, C), 49 ** -0.5, 0.875)
    ln_gain = jnp.clip(1.0 + 0.18 * jax.random.normal(splits[3], (C,), jnp.float32), 0.1, 1.9)
    ln_shift = centred(splits[4], (C,), 0.5, 3.0, (), jnp.float32)
    w_in = centred(splits[5], (C, HID), C ** -0.5, 0.375)
    w_out = centred(splits[6], (HID, C), HID ** -0.5, 0.1875)
    edge_tile = draw_edge_tile(jax.random.fold_in(splits[11], 71), 0)
    edge_code = draw_edge_code(jax.random.fold_in(splits[11], 71), 0)
    corner_tile = draw_corner_tile(jax.random.fold_in(splits[11], 71), 0)
    corner_code = draw_corner_code(jax.random.fold_in(splits[11], 71), 0)
    return {"fields": fields, "out_grad": out_grad, "kernel": kernel, "ln_gain": ln_gain, "ln_shift": ln_shift, "w_in": w_in, "w_out": w_out, "edge_tile": edge_tile, "edge_code": edge_code, "corner_tile": corner_tile, "corner_code": corner_code}


def bands_of(patches):
    edge_bands = jnp.stack([jnp.rot90(patches, e, axes=(1, 2))[:, 0:3] for e in range(4)], axis=1)
    corner_blocks = jnp.stack([jnp.rot90(patches, e, axes=(1, 2))[:, 0:3, 0:3] for e in range(4)], axis=1)
    return (edge_bands, corner_blocks)

def edge_pieces(fetched, code_table):
    is_flipped = (code_table // 4)[:, :, None, None, None] == 1
    return jnp.where(is_flipped, fetched[:, :, :, ::-1], fetched)[:, :, ::-1]

def corner_pieces(fetched, code_table):
    is_transposed = (code_table // 4)[:, :, None, None, None] == 1
    return jnp.where(is_transposed, jnp.swapaxes(fetched, 2, 3), fetched)[:, :, ::-1, ::-1]

def edge_return(rim_bands, code_table):
    is_flipped = (code_table // 4)[:, :, None, None, None] == 1
    restored = rim_bands[:, :, ::-1]
    return jnp.where(is_flipped, restored[:, :, :, ::-1], restored)

def corner_return(rim_bands, code_table):
    is_transposed = (code_table // 4)[:, :, None, None, None] == 1
    restored = rim_bands[:, :, ::-1, ::-1]
    return jnp.where(is_transposed, jnp.swapaxes(restored, 2, 3), restored)

def assemble(patches, edge_halo, corner_halo):
    extent = patches.shape[1]
    padded = jnp.zeros((patches.shape[0], extent + 6, extent + 6, patches.shape[3]), patches.dtype)
    padded = padded.at[:, 3:extent + 3, 3:extent + 3].set(patches)
    for e in range(4):
        turned = jnp.rot90(padded, e, axes=(1, 2))
        turned = turned.at[:, 0:3, 3:extent + 3].set(edge_halo[:, e])
        turned = turned.at[:, 0:3, 0:3].set(corner_halo[:, e])
        padded = jnp.rot90(turned, -e, axes=(1, 2))
    return padded

def split_rims(grad_padded):
    extent = grad_padded.shape[1] - 6
    edge_rims = []
    corner_rims = []
    for e in range(4):
        turned = jnp.rot90(grad_padded, e, axes=(1, 2))
        edge_rims.append(turned[:, 0:3, 3:extent + 3])
        corner_rims.append(turned[:, 0:3, 0:3])
    interior = grad_padded[:, 3:extent + 3, 3:extent + 3]
    return (jnp.stack(edge_rims, axis=1), jnp.stack(corner_rims, axis=1), interior)

def place_rims(running, edge_grads, corner_grads):
    for e in range(4):
        turned = jnp.rot90(running, e, axes=(1, 2))
        turned = turned.at[:, 0:3].add(edge_grads[:, e])
        turned = turned.at[:, 0:3, 0:3].add(corner_grads[:, e])
        running = jnp.rot90(turned, -e, axes=(1, 2))
    return running

def depthwise(padded, kernel):
    extent = padded.shape[1] - 6
    widened = padded.astype(jnp.float32)
    kernel_f = kernel.astype(jnp.float32)
    running = jnp.zeros((padded.shape[0], extent, extent, padded.shape[3]), jnp.float32)
    for a in range(7):
        for b in range(7):
            running = running + kernel_f[a, b] * widened[:, a:a + extent, b:b + extent]
    return running

def kernel_grad(padded, grad_z):
    extent = grad_z.shape[1]
    widened = padded.astype(jnp.float32)
    pieces = []
    for a in range(7):
        for b in range(7):
            pieces.append(lax.optimization_barrier(jnp.sum(grad_z * widened[:, a:a + extent, b:b + extent], axis=(0, 1, 2))))
    return jnp.stack(pieces, axis=0).reshape(7, 7, grad_z.shape[3])

def input_grad(grad_z, kernel):
    extent = grad_z.shape[1]
    kernel_f = kernel.astype(jnp.float32)
    padded_grad = jnp.pad(grad_z, ((0, 0), (6, 6), (6, 6), (0, 0)))
    running = jnp.zeros((grad_z.shape[0], extent + 6, extent + 6, grad_z.shape[3]), jnp.float32)
    for a in range(7):
        for b in range(7):
            running = running + kernel_f[a, b] * padded_grad[:, 6 - a:12 - a + extent, 6 - b:12 - b + extent]
    return running

def gelu_parts(hidden):
    normal_cdf = 0.5 * (1.0 + jax.scipy.special.erf(hidden / math.sqrt(2.0)))
    normal_pdf = jnp.exp(-0.5 * hidden * hidden) / math.sqrt(2.0 * math.pi)
    return (hidden * normal_cdf, normal_cdf + hidden * normal_pdf)

def block(padded, patches, cotangent, kernel, ln_gain, ln_shift, w_in, w_out):
    z_field = depthwise(padded, kernel)
    channels = z_field.shape[3]
    flat_z = z_field.reshape(-1, channels)
    average = lax.optimization_barrier(jnp.mean(flat_z, axis=1, keepdims=True))
    centered = flat_z - average
    variance = lax.optimization_barrier(jnp.mean(centered * centered, axis=1, keepdims=True))
    inv_std = lax.rsqrt(variance + 1e-06)
    normed = centered * inv_std
    zn_rows = (normed * ln_gain + ln_shift).astype(jnp.bfloat16)
    hidden = jnp.dot(zn_rows, w_in, preferred_element_type=jnp.float32)
    activ, gelu_slope = gelu_parts(hidden)
    activated = activ.astype(jnp.bfloat16)
    branch_out = jnp.dot(activated, w_out, preferred_element_type=jnp.float32)
    outcome = (patches.reshape(-1, channels).astype(jnp.float32) + branch_out).astype(jnp.bfloat16)
    cot_rows = cotangent.reshape(-1, channels)
    grad_wout = jnp.dot(activated.T, cot_rows, preferred_element_type=jnp.float32)
    grad_act = jnp.dot(cot_rows, w_out.T, preferred_element_type=jnp.float32)
    grad_hidden = (grad_act * gelu_slope).astype(jnp.bfloat16)
    grad_win = jnp.dot(zn_rows.T, grad_hidden, preferred_element_type=jnp.float32)
    grad_normed = jnp.dot(grad_hidden, w_in.T, preferred_element_type=jnp.float32)
    grad_gain = lax.optimization_barrier(jnp.sum(grad_normed * normed, axis=0))
    grad_shift = lax.optimization_barrier(jnp.sum(grad_normed, axis=0))
    scaled = grad_normed * ln_gain
    grad_z = inv_std * (scaled - lax.optimization_barrier(jnp.mean(scaled, axis=1, keepdims=True)) - normed * lax.optimization_barrier(jnp.mean(scaled * normed, axis=1, keepdims=True)))
    grad_z = grad_z.reshape(z_field.shape)
    grads = (kernel_grad(padded, grad_z), grad_gain, grad_shift, grad_win, grad_wout)
    return (outcome.reshape(patches.shape), input_grad(grad_z, kernel), grads)

def per_replica(patches, cotangent, kernel, ln_gain, ln_shift, w_in, w_out, edge_tile, edge_code, corner_tile, corner_code):
    tile_count = patches.shape[0]
    edge_bands, corner_blocks = bands_of(patches)
    edge_src = (edge_tile * 4 + edge_code % 4).astype(jnp.int32)
    corner_src = (corner_tile * 4 + corner_code % 4).astype(jnp.int32)
    fetched_edge = edge_bands.reshape((tile_count * 4,) + edge_bands.shape[2:])[edge_src]
    fetched_corner = corner_blocks.reshape((tile_count * 4,) + corner_blocks.shape[2:])[corner_src]
    padded = assemble(patches, edge_pieces(fetched_edge, edge_code), corner_pieces(fetched_corner, corner_code))
    outcome, grad_padded, grads = block(padded, patches, cotangent, kernel, ln_gain, ln_shift, w_in, w_out)
    edge_rims, corner_rims, interior = split_rims(grad_padded)
    back_edge = edge_return(edge_rims, edge_code).reshape((tile_count * 4,) + edge_rims.shape[2:])
    back_corner = corner_return(corner_rims, corner_code).reshape((tile_count * 4,) + corner_rims.shape[2:])
    edge_sums = jax.ops.segment_sum(back_edge, edge_src.reshape(-1), num_segments=tile_count * 4).reshape(edge_rims.shape)
    corner_sums = jax.ops.segment_sum(back_corner, corner_src.reshape(-1), num_segments=tile_count * 4).reshape(corner_rims.shape)
    running = place_rims(interior + cotangent.astype(jnp.float32), edge_sums, corner_sums)
    return (outcome, running.astype(jnp.bfloat16), grads)

def reference(fields, out_grad, kernel, ln_gain, ln_shift, w_in, w_out, edge_tile, edge_code, corner_tile, corner_code):

    def member_step(members):
        return per_replica(members[0], members[1], kernel, ln_gain, ln_shift, w_in, w_out, edge_tile, edge_code, corner_tile, corner_code)
    outcome, grad_input, grads = lax.map(member_step, (fields, out_grad))
    norm_scale = 1.0 / math.sqrt(REPS * TILES * P_SIZE * P_SIZE)
    return (outcome, grad_input, lax.optimization_barrier(jnp.sum(grads[0], axis=0)) * norm_scale, lax.optimization_barrier(jnp.sum(grads[1], axis=0)) * norm_scale, lax.optimization_barrier(jnp.sum(grads[2], axis=0)) * norm_scale, lax.optimization_barrier(jnp.sum(grads[3], axis=0)) * norm_scale, lax.optimization_barrier(jnp.sum(grads[4], axis=0)) * norm_scale)
```

```python
import math

import jax
import jax.numpy as jnp
from jax import lax
from jax.sharding import PartitionSpec as P


def for_sending(array):
    return jax.tree.map(lambda a: a.astype(jnp.bfloat16) if a.dtype == jnp.float32 else a, array)


def bands_of(patches):
    edge_bands = jnp.stack([jnp.rot90(patches, e, axes=(1, 2))[:, 0:3] for e in range(4)], axis=1)
    corner_blocks = jnp.stack(
        [jnp.rot90(patches, e, axes=(1, 2))[:, 0:3, 0:3] for e in range(4)], axis=1
    )
    return (edge_bands, corner_blocks)


def edge_pieces(fetched, code_table):
    is_flipped = (code_table // 4)[:, :, None, None, None] == 1
    return jnp.where(is_flipped, fetched[:, :, :, ::-1], fetched)[:, :, ::-1]


def corner_pieces(fetched, code_table):
    is_transposed = (code_table // 4)[:, :, None, None, None] == 1
    return jnp.where(is_transposed, jnp.swapaxes(fetched, 2, 3), fetched)[:, :, ::-1, ::-1]


def edge_return(rim_bands, code_table):
    is_flipped = (code_table // 4)[:, :, None, None, None] == 1
    restored = rim_bands[:, :, ::-1]
    return jnp.where(is_flipped, restored[:, :, :, ::-1], restored)


def corner_return(rim_bands, code_table):
    is_transposed = (code_table // 4)[:, :, None, None, None] == 1
    restored = rim_bands[:, :, ::-1, ::-1]
    return jnp.where(is_transposed, jnp.swapaxes(restored, 2, 3), restored)


def assemble(patches, edge_halo, corner_halo):
    extent = patches.shape[1]
    padded = jnp.zeros((patches.shape[0], extent + 6, extent + 6, patches.shape[3]), patches.dtype)
    padded = padded.at[:, 3 : extent + 3, 3 : extent + 3].set(patches)
    for e in range(4):
        turned = jnp.rot90(padded, e, axes=(1, 2))
        turned = turned.at[:, 0:3, 3 : extent + 3].set(edge_halo[:, e])
        turned = turned.at[:, 0:3, 0:3].set(corner_halo[:, e])
        padded = jnp.rot90(turned, -e, axes=(1, 2))
    return padded


def split_rims(grad_padded):
    extent = grad_padded.shape[1] - 6
    edge_rims = []
    corner_rims = []
    for e in range(4):
        turned = jnp.rot90(grad_padded, e, axes=(1, 2))
        edge_rims.append(turned[:, 0:3, 3 : extent + 3])
        corner_rims.append(turned[:, 0:3, 0:3])
    interior = grad_padded[:, 3 : extent + 3, 3 : extent + 3]
    return (jnp.stack(edge_rims, axis=1), jnp.stack(corner_rims, axis=1), interior)


def place_rims(running, edge_grads, corner_grads):
    for e in range(4):
        turned = jnp.rot90(running, e, axes=(1, 2))
        turned = turned.at[:, 0:3].add(edge_grads[:, e])
        turned = turned.at[:, 0:3, 0:3].add(corner_grads[:, e])
        running = jnp.rot90(turned, -e, axes=(1, 2))
    return running


def depthwise(padded, kernel):
    extent = padded.shape[1] - 6
    widened = padded.astype(jnp.float32)
    kernel_f = kernel.astype(jnp.float32)
    running = jnp.zeros((padded.shape[0], extent, extent, padded.shape[3]), jnp.float32)
    for a in range(7):
        for b in range(7):
            running = running + kernel_f[a, b] * widened[:, a : a + extent, b : b + extent]
    return running


def kernel_grad(padded, grad_z):
    extent = grad_z.shape[1]
    widened = padded.astype(jnp.float32)
    pieces = []
    for a in range(7):
        for b in range(7):
            pieces.append(
                jnp.sum(grad_z * widened[:, a : a + extent, b : b + extent], axis=(0, 1, 2))
            )
    return jnp.stack(pieces, axis=0).reshape(7, 7, grad_z.shape[3])


def input_grad(grad_z, kernel):
    extent = grad_z.shape[1]
    kernel_f = kernel.astype(jnp.float32)
    padded_grad = jnp.pad(grad_z, ((0, 0), (6, 6), (6, 6), (0, 0)))
    running = jnp.zeros((grad_z.shape[0], extent + 6, extent + 6, grad_z.shape[3]), jnp.float32)
    for a in range(7):
        for b in range(7):
            running = (
                running
                + kernel_f[a, b] * padded_grad[:, 6 - a : 12 - a + extent, 6 - b : 12 - b + extent]
            )
    return running


def gelu_parts(hidden):
    normal_cdf = 0.5 * (1.0 + jax.scipy.special.erf(hidden / math.sqrt(2.0)))
    normal_pdf = jnp.exp(-0.5 * hidden * hidden) / math.sqrt(2.0 * math.pi)
    return (hidden * normal_cdf, normal_cdf + hidden * normal_pdf)


def block(padded, patches, cotangent, kernel, ln_gain, ln_shift, w_in, w_out):
    z_field = depthwise(padded, kernel)
    channels = z_field.shape[3]
    flat_z = z_field.reshape(-1, channels)
    average = jnp.mean(flat_z, axis=1, keepdims=True)
    centered = flat_z - average
    variance = jnp.mean(centered * centered, axis=1, keepdims=True)
    inv_std = lax.rsqrt(variance + 1e-06)
    normed = centered * inv_std
    zn_rows = (normed * ln_gain + ln_shift).astype(jnp.bfloat16)
    hidden = jnp.dot(zn_rows, w_in, preferred_element_type=jnp.float32)
    activ, gelu_slope = gelu_parts(hidden)
    activated = activ.astype(jnp.bfloat16)
    branch_out = jnp.dot(activated, w_out, preferred_element_type=jnp.float32)
    outcome = (patches.reshape(-1, channels).astype(jnp.float32) + branch_out).astype(jnp.bfloat16)
    cot_rows = cotangent.reshape(-1, channels)
    grad_wout = jnp.dot(activated.T, cot_rows, preferred_element_type=jnp.float32)
    grad_act = jnp.dot(cot_rows, w_out.T, preferred_element_type=jnp.float32)
    grad_hidden = (grad_act * gelu_slope).astype(jnp.bfloat16)
    grad_win = jnp.dot(zn_rows.T, grad_hidden, preferred_element_type=jnp.float32)
    grad_normed = jnp.dot(grad_hidden, w_in.T, preferred_element_type=jnp.float32)
    grad_gain = jnp.sum(grad_normed * normed, axis=0)
    grad_shift = jnp.sum(grad_normed, axis=0)
    scaled = grad_normed * ln_gain
    grad_z = inv_std * (
        scaled
        - jnp.mean(scaled, axis=1, keepdims=True)
        - normed * jnp.mean(scaled * normed, axis=1, keepdims=True)
    )
    grad_z = grad_z.reshape(z_field.shape)
    grads = (kernel_grad(padded, grad_z), grad_gain, grad_shift, grad_win, grad_wout)
    return (outcome.reshape(patches.shape), input_grad(grad_z, kernel), grads)


def chunked(bands, corners):
    parts = lax.axis_size("face")
    tiles, channels = bands.shape[0], bands.shape[-1]
    span = bands.shape[3] // parts
    band_part = bands.reshape(tiles * 4, 3, parts, span, channels)
    band_part = band_part.transpose(2, 0, 3, 1, 4).reshape(parts, tiles * 4, span * 3 * channels)
    corner_part = corners.reshape(tiles * 4, 9, channels).transpose(1, 0, 2)
    corner_part = jnp.pad(corner_part, ((0, parts - 9), (0, 0), (0, channels)))
    return jnp.concatenate([band_part, corner_part], axis=2)


def unchunked(parts_array, tiles):
    parts, _, width = parts_array.shape
    channels = width // 8
    span = 6 // 3
    band_part = parts_array[:, :, : 6 * channels].reshape(parts, tiles * 4, span, 3, channels)
    bands = band_part.transpose(1, 3, 0, 2, 4).reshape(tiles, 4, 3, parts * span, channels)
    corners = parts_array[:9, :, 6 * channels : 7 * channels].transpose(1, 0, 2)
    return bands, corners.reshape(tiles, 4, 3, 3, channels)


def swap_face(array):
    return lax.all_to_all(array, "face", 0, 0, tiled=True)


def routed(bands, corners, pick_edge, pick_corner):
    tiles = bands.shape[0]
    sent = swap_face(chunked(bands.astype(jnp.bfloat16), corners.astype(jnp.bfloat16)))
    width = sent.shape[2] * 6 // 8
    rows = sent.reshape(-1, sent.shape[2])
    chosen = jnp.concatenate(
        [
            jnp.dot(pick_edge, rows[:, :width], preferred_element_type=jnp.float32),
            jnp.dot(pick_corner, rows[:, width:], preferred_element_type=jnp.float32),
        ],
        axis=1,
    ).astype(jnp.bfloat16)
    return unchunked(swap_face(chosen.reshape(sent.shape)), tiles)


def body(
    fields,
    out_grad,
    kernel,
    ln_gain,
    ln_shift,
    w_in,
    w_out,
    edge_tile,
    edge_code,
    corner_tile,
    corner_code,
):
    patches = fields[0]
    cotangent = out_grad[0]
    tile_count = patches.shape[0]
    extent = patches.shape[1]
    channels = patches.shape[-1]
    faces = lax.axis_size("face")
    reps = lax.axis_size("rep")
    offset = lax.axis_index("face") * tile_count
    slot_ids = jnp.arange(tile_count * 4 * faces, dtype=jnp.int32)
    edge_src = (edge_tile * 4 + edge_code % 4).reshape(-1)
    corner_src = (corner_tile * 4 + corner_code % 4).reshape(-1)
    pick_edge = (edge_src[:, None] == slot_ids[None, :]).astype(jnp.bfloat16)
    pick_corner = (corner_src[:, None] == slot_ids[None, :]).astype(jnp.bfloat16)
    my_edge_code = lax.dynamic_slice_in_dim(edge_code, offset, tile_count, 0)
    my_corner_code = lax.dynamic_slice_in_dim(corner_code, offset, tile_count, 0)

    edge_bands, corner_blocks = bands_of(patches)
    fetched_edge, fetched_corner = routed(edge_bands, corner_blocks, pick_edge, pick_corner)
    padded = assemble(
        patches,
        edge_pieces(fetched_edge, my_edge_code),
        corner_pieces(fetched_corner, my_corner_code),
    )
    outcome, grad_padded, grads = block(
        padded, patches, cotangent, kernel, ln_gain, ln_shift, w_in, w_out
    )
    edge_rims, corner_rims, interior = split_rims(grad_padded)
    edge_sums, corner_sums = routed(
        edge_return(edge_rims, my_edge_code),
        corner_return(corner_rims, my_corner_code),
        pick_edge.T,
        pick_corner.T,
    )
    running = place_rims(
        interior + cotangent.astype(jnp.float32),
        edge_sums.astype(jnp.float32),
        corner_sums.astype(jnp.float32),
    )
    norm_scale = 1.0 / math.sqrt(reps * faces * tile_count * extent * extent)

    devices = faces * reps
    both = ("face", "rep")
    wide = jnp.concatenate(
        [grads[3].reshape(devices, -1, channels), grads[4].reshape(devices, -1, channels)], axis=1
    ).astype(jnp.bfloat16)
    wide = lax.all_to_all(wide, both, 0, 0, tiled=True)
    wide = jnp.sum(wide.astype(jnp.float32), axis=0, keepdims=True) * norm_scale
    wide = jnp.broadcast_to(wide.astype(jnp.bfloat16), (devices,) + wide.shape[1:])
    wide = lax.all_to_all(wide, both, 0, 0, tiled=True).astype(jnp.float32)
    half = wide.shape[1] // 2
    grad_win = wide[:, :half].reshape(grads[3].shape)
    grad_wout = wide[:, half:].reshape(grads[4].shape)

    small = jnp.concatenate(
        [grads[0].reshape(-1, channels), grads[1][None], grads[2][None]], axis=0
    )
    count = small.shape[0]
    small = jnp.pad(small, ((0, -count % 16), (0, 0))).astype(jnp.bfloat16)
    for axis, size in (("face", faces), ("rep", reps)):
        small = jnp.broadcast_to(small.astype(jnp.bfloat16)[None], (size,) + small.shape)
        small = lax.all_to_all(small, axis, 0, 0, tiled=True)
        small = jnp.sum(small.astype(jnp.float32), axis=0)
    small = small * norm_scale
    return (
        outcome[None],
        running.astype(jnp.bfloat16)[None],
        small[: count - 2].reshape(kernel.shape),
        small[count - 2],
        small[count - 1],
        grad_win,
        grad_wout,
    )


def solution(mesh):
    return jax.shard_map(
        body,
        mesh=mesh,
        in_specs=(
            P("rep", "face", None, None, None),
            P("rep", "face", None, None, None),
            P(),
            P(),
            P(),
            P(),
            P(),
            P(),
            P(),
            P(),
            P(),
        ),
        out_specs=(
            P("rep", "face", None, None, None),
            P("rep", "face", None, None, None),
            P(),
            P(),
            P(),
            P(),
            P(),
        ),
        check_vma=False,
    )
```

```python
import functools
import math

import jax
import jax.numpy as jnp
import numpy as np
from jax import lax
from jax.experimental import pallas as pl
from jax.experimental.pallas import tpu as pltpu
from jax.sharding import PartitionSpec as P

BF = jnp.bfloat16
F32 = jnp.float32
N = 32
J = 16
C = 256
HALF = 128
HID = 1024
T = 2
PARTS = 16
KB = 8
CANVAS = 64
RIMS = 2 * 3 * CANVAS + 2 * N * 16
VMEM_LIMIT = 60 * 1024 * 1024


def band_pixel(e, r, p):
    return ((r, p), (p, N - 1 - r), (N - 1 - r, N - 1 - p), (N - 1 - p, r))[e]


def turned_pixel(e, i, j):
    last = N + 5
    return ((i, j), (j, last - i), (last - i, last - j), (last - j, i))[e]


def chunk_row(e, r, p):
    return (p // 2) * 4 * KB + e * KB + (p % 2) * 3 + r


def corner_row(e, r, c):
    return (r * 3 + c) * 4 * KB + e * KB + 6


def band_selector():
    sel = np.zeros((PARTS * 4 * KB, N * N), np.float32)
    for e in range(4):
        for r in range(3):
            for p in range(N):
                y, x = band_pixel(e, r, p)
                sel[chunk_row(e, r, p), y * N + x] = 1
            for c in range(3):
                y, x = band_pixel(e, r, c)
                sel[corner_row(e, r, c), y * N + x] = 1
    return sel


def rim_sources():
    table = {}
    for e in range(4):
        for i in range(3):
            for j in range(N):
                pixel = turned_pixel(e, i, j + 3)
                table[pixel] = (e, chunk_row(e, 2 - i, j), chunk_row(e, 2 - i, N - 1 - j))
            for j in range(3):
                pixel = turned_pixel(e, i, j)
                table[pixel] = (
                    4 + e,
                    corner_row(e, 2 - i, 2 - j),
                    corner_row(e, 2 - j, 2 - i),
                )
    return table


def tables_of(pixels):
    table = rim_sources()
    piece = np.zeros((len(pixels), 8), np.int32)
    plain = np.full((len(pixels),), -1, np.int32)
    flipped = np.full((len(pixels),), -1, np.int32)
    for row, pixel in enumerate(pixels):
        if pixel in table:
            which, plain[row], flipped[row] = table[pixel]
            piece[row, which] = 1
    return piece, plain, flipped


def forward_rim_pixels():
    rows = [(p, q - 13) for p in (0, 1, 2, 35, 36, 37) for q in range(CANVAS)]
    rows += [(p, q - 13) for p in range(3, 35) for q in range(16)]
    rows += [(p, q - 13) for p in range(3, 35) for q in range(48, 64)]
    return rows


RIM_PAIRS = (-2, -1, 16, 17)


def backward_rim_pixels():
    rows = [(p, 3 + 2 * j + u) for p in (0, 1, 2, 35, 36, 37) for u in range(2) for j in range(J)]
    rows += [
        (2 * k + v, 3 + 2 * j + u)
        for k in range(19)
        for u in range(2)
        for v in range(2)
        for j in RIM_PAIRS
    ]
    rows += [(-9, -9)] * (512 - len(rows))
    return rows


def one_hot_rows(tables, flags, width):
    piece, plain, flipped = tables
    is_flipped = jnp.sum(piece[None] * flags[:, None, :], axis=2) > 0
    index = jnp.where(is_flipped, flipped[None], plain[None])
    return (index[:, :, None] == jnp.arange(width, dtype=jnp.int32)).astype(BF)


def pair_selector():
    sel = np.zeros((128, CANVAS), np.float32)
    for d in range(4):
        for s in range(2):
            for j in range(J):
                sel[d * 32 + s * 16 + j, 13 + 2 * (j + d) + s] = 1
    return sel


def grad_pair_selector():
    sel = np.zeros((128, 32), np.float32)
    for d in range(4):
        for s in range(2):
            for j in range(J):
                col = 2 * (j + d) + s - 3
                if 0 <= col < N:
                    sel[d * 32 + s * 16 + j, (col % 2) * 16 + col // 2] = 1
    return sel


def grad_rim_selector():
    sel = np.zeros((128, 128), np.float32)
    for d in range(4):
        for s in range(2):
            for v in range(2):
                for t in range(T):
                    for at, j in enumerate(RIM_PAIRS):
                        col = 2 * (j + d) + s - 3
                        if 0 <= col < N:
                            row = (d * 2 + s) * 16 + v * 8 + t * 4 + at
                            sel[row, v * 64 + t * 32 + (col % 2) * 16 + col // 2] = 1
    return sel


def split_columns():
    sel = np.zeros((256, 256), np.float32)
    for r in range(8):
        for col in range(N):
            sel[r * 32 + (col % 2) * 16 + col // 2, r * 32 + col] = 1
    return sel


def dot(a, b):
    return jnp.dot(a, b, preferred_element_type=F32)


def pack_kernel(fields_ref, sel_ref, out_ref):
    for t in range(T):
        x = fields_ref[t].reshape(N * N, C)
        rows = dot(sel_ref[...], x).astype(BF)
        out_ref[:, t * 32 : (t + 1) * 32, :] = rows.reshape(PARTS, 32, C)


def build_weights(kern_ref, w_ref, mirrored):
    eye = lax.broadcasted_iota(jnp.int32, (HALF, HALF), 0) == lax.broadcasted_iota(
        jnp.int32, (HALF, HALF), 1
    )
    zero = jnp.zeros((HALF, HALF), BF)

    def step(a, carry):
        row = 6 - a if mirrored else a
        taps = kern_ref[row]
        for h in range(2):
            blocks = [
                jnp.where(eye, taps[b : b + 1, h * HALF : (h + 1) * HALF], 0.0).astype(BF)
                for b in range(7)
            ]
            if mirrored:
                blocks = blocks[::-1]
            for d in range(4):
                for s in range(2):
                    for u in range(2):
                        b = 2 * d + s - u
                        block = blocks[b] if 0 <= b <= 6 else zero
                        top = d * 256 + s * HALF
                        w_ref[h, a, top : top + HALF, u * HALF : (u + 1) * HALF] = block
        return carry

    lax.fori_loop(0, 7, step, 0)


def spread(picked, q_ref, index, base):
    rows = picked.shape[0] // 8
    for d in range(4):
        for s in range(2):
            at = (d * 2 + s) * rows
            for h in range(2):
                lane = d * 256 + s * HALF
                q_ref[h, index, base : base + rows, lane : lane + HALF] = picked[
                    at : at + rows, h * HALF : (h + 1) * HALF
                ]


def forward_kernel(
    fields_ref,
    og_ref,
    recv_ref,
    rim_ref,
    kern_ref,
    gain_ref,
    shift_ref,
    win_ref,
    wout_ref,
    win_t_ref,
    wout_t_ref,
    psel_ref,
    split_ref,
    merge_ref,
    result_ref,
    wide_ref,
    gz_ref,
    gains_ref,
    q_out_ref,
    pad_ref,
    q_ref,
    w_ref,
    x_ref,
    o_ref,
    z_ref,
    gwin_ref,
    gwout_ref,
    sem,
):
    build_weights(kern_ref, w_ref, False)
    for t in range(T):
        recv = recv_ref[:, t * 32 : (t + 1) * 32, :].reshape(512, C)
        rims = dot(rim_ref[t], recv).astype(BF)
        rows = 3 * CANVAS
        pad_ref[t, 0:3] = rims[:rows].reshape(3, CANVAS, C)
        pad_ref[t, 35:38] = rims[rows : 2 * rows].reshape(3, CANVAS, C)
        pad_ref[t, 3:35, 0:16] = rims[2 * rows : 2 * rows + 512].reshape(N, 16, C)
        pad_ref[t, 3:35, 48:64] = rims[2 * rows + 512 :].reshape(N, 16, C)
        pad_ref[t, 3:35, 16:48] = fields_ref[t]

    def pairs(row, carry):
        for t in range(T):
            picked = dot(psel_ref[...], pad_ref[t, row]).astype(BF)
            spread(picked, q_ref, row, t * 16)
        return carry

    lax.fori_loop(0, N + 6, pairs, 0)
    copy = pltpu.make_async_copy(q_ref, q_out_ref, sem)
    copy.start()

    def order(m, carry):
        for t in range(T):
            rows = pl.ds(m * 8, 8)
            for src, dst in ((fields_ref, x_ref), (og_ref, o_ref)):
                block = src[t, rows].reshape(256, C)
                dst[rows, t * 32 : (t + 1) * 32] = (
                    dot(split_ref[...], block).astype(BF).reshape(8, 32, C)
                )
        return carry

    lax.fori_loop(0, 4, order, 0)

    def conv(m, carry):
        for h in range(2):
            acc = None
            for a in range(7):
                lhs = q_ref[h, pl.ds(m * 8 + a, 8)].reshape(256, 1024)
                part = dot(lhs, w_ref[h, a])
                acc = part if acc is None else acc + part
            acc = acc.reshape(8, T, 16, 256)
            for t in range(T):
                for u in range(2):
                    base = t * 32 + u * 16
                    z_ref[
                        pl.ds(m * 8, 8), base : base + 16, h * HALF : (h + 1) * HALF
                    ] = acc[:, t, :, u * HALF : (u + 1) * HALF]
        return carry

    lax.fori_loop(0, 4, conv, 0)

    gwin_ref[...] = jnp.zeros_like(gwin_ref)
    gwout_ref[...] = jnp.zeros_like(gwout_ref)
    gains_ref[...] = jnp.zeros_like(gains_ref)
    gain = gain_ref[...]
    shift = shift_ref[...]

    def mlp(m, carry):
        rows = pl.ds(m * 4, 4)
        z = z_ref[rows].reshape(256, C)
        average = jnp.mean(z, axis=1, keepdims=True)
        centered = z - average
        variance = jnp.mean(centered * centered, axis=1, keepdims=True)
        inv_std = lax.rsqrt(variance + 1e-06)
        normed = centered * inv_std
        zn = (normed * gain + shift).astype(BF)
        og = o_ref[rows].reshape(256, C)
        hidden = dot(zn, win_ref[...])
        cdf = 0.5 * (1.0 + lax.erf(hidden * (1.0 / math.sqrt(2.0))))
        pdf = jnp.exp(-0.5 * hidden * hidden) * (1.0 / math.sqrt(2.0 * math.pi))
        act = (hidden * cdf).astype(BF)
        slope = cdf + hidden * pdf
        out = x_ref[rows].reshape(256, C).astype(F32) + dot(act, wout_ref[...])
        x_ref[rows] = out.astype(BF).reshape(4, 64, C)
        grad_hidden = (dot(og, wout_t_ref[...]) * slope).astype(BF)
        gwout_ref[...] += dot(og.T, act)
        gwin_ref[...] += dot(zn.T, grad_hidden)
        grad_normed = dot(grad_hidden, win_t_ref[...])
        gains_ref[0:8] += jnp.sum((grad_normed * normed).reshape(32, 8, C), axis=0)
        gains_ref[8:16] += jnp.sum(grad_normed.reshape(32, 8, C), axis=0)
        scaled = grad_normed * gain
        grad_z = inv_std * (
            scaled
            - jnp.mean(scaled, axis=1, keepdims=True)
            - normed * jnp.mean(scaled * normed, axis=1, keepdims=True)
        )
        gz_ref[rows] = grad_z.astype(BF).reshape(4, 64, C)
        return carry

    lax.fori_loop(0, 8, mlp, 0)

    def unorder(m, carry):
        for t in range(T):
            rows = pl.ds(m * 8, 8)
            block = x_ref[rows, t * 32 : (t + 1) * 32].reshape(256, C)
            result_ref[t, rows] = dot(merge_ref[...], block).astype(BF).reshape(8, 32, C)
        return carry

    lax.fori_loop(0, 4, unorder, 0)
    wide_ref[:, 0:8] = gwout_ref[...].T.reshape(128, 8, C).astype(BF)
    wide_ref[:, 8:16] = gwin_ref[...].T.reshape(128, 8, C).astype(BF)
    copy.wait()


def backward_kernel(
    gz_ref,
    q_in_ref,
    kern_ref,
    rim_t_ref,
    gsel_ref,
    rsel_ref,
    sent_ref,
    inner_ref,
    taps_ref,
    q_ref,
    w_ref,
    g_ref,
    r_ref,
    gt_ref,
    edge_ref,
    sem,
):
    copy = pltpu.make_async_copy(q_in_ref, q_ref, sem)
    copy.start()
    build_weights(kern_ref, w_ref, True)
    zeros = jnp.zeros((6, 32, 1024), BF)
    for h in range(2):
        g_ref[h, 0:6] = zeros
        g_ref[h, 38:44] = zeros
        r_ref[0, h, 0:3] = jnp.zeros((3, 16, 1024), BF)
        r_ref[0, h, 19:22] = jnp.zeros((3, 16, 1024), BF)
        r_ref[1, h, 0:2] = jnp.zeros((2, 16, 1024), BF)
        r_ref[1, h, 19:22] = jnp.zeros((3, 16, 1024), BF)

    def pairs(i, carry):
        for v in range(2):
            for t in range(T):
                block = gz_ref[2 * i + v, t * 32 : (t + 1) * 32]
                spread(dot(gsel_ref[...], block).astype(BF), g_ref, 6 + 2 * i + v, t * 16)
        spread(
            dot(rsel_ref[...], gz_ref[pl.ds(2 * i, 2)].reshape(128, C)).astype(BF),
            r_ref.at[0],
            3 + i,
            0,
        )
        return carry

    lax.fori_loop(0, 16, pairs, 0)

    def odd_pairs(i, carry):
        spread(
            dot(rsel_ref[...], gz_ref[pl.ds(2 * i + 1, 2)].reshape(128, C)).astype(BF),
            r_ref.at[1],
            3 + i,
            0,
        )
        return carry

    lax.fori_loop(0, 15, odd_pairs, 0)
    blank = jnp.zeros((64, C), BF)
    first = jnp.concatenate([blank, gz_ref[0]], axis=0)
    spread(dot(rsel_ref[...], first).astype(BF), r_ref.at[1], 2, 0)
    last = jnp.concatenate([gz_ref[31], blank], axis=0)
    spread(dot(rsel_ref[...], last).astype(BF), r_ref.at[1], 18, 0)

    for h in range(2):
        acc = None
        for a in range(7):
            k, v = a // 2, a % 2
            part = dot(r_ref[v, h, k : k + 19].reshape(304, 1024), w_ref[h, a])
            acc = part if acc is None else acc + part
        acc = acc.astype(BF).reshape(19, 16, 256)
        edge_ref[h, 192:496] = acc.reshape(304, 256)

    for h in range(2):
        for base, at in ((0, 0), (35, 96)):
            acc = None
            for a in range(7):
                lhs = g_ref[h, base + a : base + a + 3].reshape(96, 1024)
                part = dot(lhs, w_ref[h, a])
                acc = part if acc is None else acc + part
            edge_ref[h, at : at + 96] = acc.astype(BF)
        edge_ref[h, 496:512] = jnp.zeros((16, 256), BF)

    edges = jnp.concatenate(
        [
            jnp.concatenate([edge_ref[0, :, 0:HALF], edge_ref[1, :, 0:HALF]], axis=1),
            jnp.concatenate([edge_ref[0, :, HALF:], edge_ref[1, :, HALF:]], axis=1),
        ],
        axis=0,
    )
    for t in range(T):
        rows = dot(rim_t_ref[t], edges).astype(BF)
        sent_ref[:, t * 32 : (t + 1) * 32, :] = rows.reshape(PARTS, 32, C)

    def inside(m, carry):
        for h in range(2):
            acc = None
            for a in range(7):
                lhs = g_ref[h, pl.ds(m * 8 + 3 + a, 8)].reshape(256, 1024)
                part = dot(lhs, w_ref[h, a])
                acc = part if acc is None else acc + part
            acc = acc.reshape(8, T, 16, 256)
            for t in range(T):
                for u in range(2):
                    inner_ref[h, t, pl.ds(m * 8, 8), pl.ds(u, 16, stride=2), :] = acc[
                        :, t, :, u * HALF : (u + 1) * HALF
                    ]
        return carry

    lax.fori_loop(0, 4, inside, 0)

    for h in range(2):
        for u in range(2):
            for t in range(T):
                block = gz_ref[:, t * 32 + u * 16 : t * 32 + u * 16 + 16, h * HALF : (h + 1) * HALF]
                g_ref[h, 0:32, t * 16 : t * 16 + 16, u * HALF : (u + 1) * HALF] = block
        gt_ref[h] = g_ref[h, 0:32, :, 0:256].reshape(1024, 256).T
    copy.wait()
    eye = lax.broadcasted_iota(jnp.int32, (HALF, HALF), 0) == lax.broadcasted_iota(
        jnp.int32, (HALF, HALF), 1
    )

    def taps(a, carry):
        for h in range(2):
            prod = dot(gt_ref[h], q_ref[h, pl.ds(a, 32)].reshape(1024, 1024))
            sums = [None] * 7
            for d in range(4):
                for s in range(2):
                    for u in range(2):
                        b = 2 * d + s - u
                        if 0 <= b <= 6:
                            lane = d * 256 + s * HALF
                            block = jnp.where(
                                eye, prod[u * HALF : (u + 1) * HALF, lane : lane + HALF], 0.0
                            )
                            sums[b] = block if sums[b] is None else sums[b] + block
            rows = [jnp.sum(block, axis=0, keepdims=True) for block in sums]
            rows.append(jnp.zeros((1, HALF), F32))
            taps_ref[a, :, h * HALF : (h + 1) * HALF] = jnp.concatenate(rows, axis=0)
        return carry

    lax.fori_loop(0, 7, taps, 0)


def final_kernel(inner_ref, og_ref, recv_ref, sel_t_ref, out_ref):
    for t in range(T):
        recv = recv_ref[:, t * 32 : (t + 1) * 32, :].reshape(512, C)
        back = dot(sel_t_ref[...], recv).reshape(N, N, C)
        inner = jnp.concatenate([inner_ref[0, t], inner_ref[1, t]], axis=2)
        out_ref[t] = (inner + og_ref[t].astype(F32) + back).astype(BF)


def call(kernel, outs, scratch=(), out_specs=None, in_specs=None):
    options = {}
    if in_specs is not None:
        options["in_specs"] = in_specs
    if out_specs is not None:
        options["out_specs"] = out_specs
    return pl.pallas_call(
        kernel,
        out_shape=outs,
        scratch_shapes=list(scratch),
        compiler_params=pltpu.CompilerParams(vmem_limit_bytes=VMEM_LIMIT),
        **options,
    )


def swap(array, axes):
    return lax.all_to_all(array, axes, 0, 0, tiled=True)


def backward_rim_tables():
    pixels, owners = [], []
    for u in range(2):
        for p in (0, 1, 2, 35, 36, 37):
            for t in range(T):
                for j in range(J):
                    pixels.append((p, 3 + 2 * j + u))
                    owners.append(t)
        for k in range(19):
            for v in range(2):
                for t in range(T):
                    for j in RIM_PAIRS:
                        pixels.append((2 * k + v, 3 + 2 * j + u))
                        owners.append(t)
        pixels += [(-9, -9)] * 16
        owners += [0] * 16
    piece, plain, flipped = tables_of(pixels)
    owners = np.array(owners)
    plains, flippeds = [], []
    for t in range(T):
        plains.append(np.where(owners == t, plain, -1))
        flippeds.append(np.where(owners == t, flipped, -1))
    return piece, np.stack(plains), np.stack(flippeds)


def body(
    fields,
    out_grad,
    kernel,
    ln_gain,
    ln_shift,
    w_in,
    w_out,
    edge_tile,
    edge_code,
    corner_tile,
    corner_code,
):
    x = fields[0]
    og = out_grad[0]
    faces = lax.axis_size("face")
    reps = lax.axis_size("rep")
    devices = faces * reps
    norm_scale = 1.0 / math.sqrt(devices * T * N * N)
    offset = lax.axis_index("face") * T
    sel = band_selector()
    vm = pl.BlockSpec(memory_space=pltpu.VMEM)
    hbm = pl.BlockSpec(memory_space=pl.ANY)
    shape = jax.ShapeDtypeStruct

    codes = jnp.concatenate([edge_code, corner_code], axis=1) // 4
    flags = lax.dynamic_slice_in_dim(codes, offset, T, 0)
    edge_rows = (edge_tile * 4 + edge_code % 4).reshape(-1, 1) * KB
    corner_rows = (corner_tile * 4 + corner_code % 4).reshape(-1, 1) * KB
    at = np.arange(KB)[None, :]
    source = jnp.where(at < 6, edge_rows + at, corner_rows + at).reshape(-1)
    every = jnp.arange(source.shape[0], dtype=jnp.int32)
    pick = (source[:, None] == every[None, :]).astype(BF)
    pick_t = (every[:, None] == source[None, :]).astype(BF)
    piece, plain, flipped = tables_of(forward_rim_pixels())
    rim = one_hot_rows((piece, plain, flipped), flags, 512)
    piece, plain, flipped = backward_rim_tables()
    is_flipped = jnp.sum(piece[None] * flags[:, None, :], axis=2) > 0
    index = jnp.where(is_flipped, flipped, plain)
    rim_t = (jnp.arange(512, dtype=jnp.int32)[None, :, None] == index[:, None, :]).astype(BF)

    taps = jnp.pad(kernel.astype(F32), ((0, 0), (0, 1), (0, 0)))

    sent = call(pack_kernel, shape((PARTS, T * 32, C), BF))(x, sel.astype(BF))
    got = swap(sent, "face")
    routed = dot(pick, got.reshape(-1, C)).astype(BF).reshape(got.shape)
    got = swap(routed, "face")

    split = split_columns()
    q_shape = (2, N + 6, 32, 1024)
    result, wide, gz, gains, q = call(
        forward_kernel,
        (
            shape((T, N, N, C), BF),
            shape((128, 16, C), BF),
            shape((N, 64, C), BF),
            shape((16, C), F32),
            shape(q_shape, BF),
        ),
        scratch=(
            pltpu.VMEM((T, N + 6, CANVAS, C), BF),
            pltpu.VMEM(q_shape, BF),
            pltpu.VMEM((2, 7, 1024, 256), BF),
            pltpu.VMEM((N, 64, C), BF),
            pltpu.VMEM((N, 64, C), BF),
            pltpu.VMEM((N, 64, C), F32),
            pltpu.VMEM((C, HID), F32),
            pltpu.VMEM((C, HID), F32),
            pltpu.SemaphoreType.DMA,
        ),
        in_specs=[vm] * 14,
        out_specs=(vm, vm, vm, vm, hbm),
    )(
        x,
        og,
        got,
        rim,
        taps,
        ln_gain[None],
        ln_shift[None],
        w_in,
        w_out,
        w_in.T,
        w_out.T,
        pair_selector().astype(BF),
        split.astype(BF),
        split.T.astype(BF),
    )

    wide = swap(wide, ("face", "rep"))
    wide = jnp.sum(wide.astype(F32), axis=0, keepdims=True) * norm_scale
    wide = jnp.broadcast_to(wide.astype(BF), (devices,) + wide.shape[1:])
    wide = swap(wide, ("face", "rep")).astype(F32)
    grad_wout = wide[:, 0:8].reshape(HID, C)
    grad_win = wide[:, 8:16].reshape(HID, C).T

    sent, inner, tap_grads = call(
        backward_kernel,
        (
            shape((PARTS, T * 32, C), BF),
            shape((2, T, N, N, HALF), F32),
            shape((7, 8, C), F32),
        ),
        scratch=(
            pltpu.VMEM(q_shape, BF),
            pltpu.VMEM((2, 7, 1024, 256), BF),
            pltpu.VMEM((2, 44, 32, 1024), BF),
            pltpu.VMEM((2, 2, 22, 16, 1024), BF),
            pltpu.VMEM((2, 256, 1024), BF),
            pltpu.VMEM((2, 512, 256), BF),
            pltpu.SemaphoreType.DMA,
        ),
        in_specs=[vm, hbm, vm, vm, vm, vm],
        out_specs=(vm, vm, vm),
    )(
        gz,
        q,
        taps,
        rim_t,
        grad_pair_selector().astype(BF),
        grad_rim_selector().astype(BF),
    )

    got = swap(sent, "face")
    routed = dot(pick_t, got.reshape(-1, C)).astype(BF).reshape(got.shape)
    got = swap(routed, "face")
    grad_input = call(final_kernel, shape((T, N, N, C), BF))(
        inner, og, got, sel.T.astype(BF)
    )

    small = jnp.concatenate(
        [
            tap_grads.reshape(56, C),
            jnp.sum(gains[0:8], axis=0, keepdims=True),
            jnp.sum(gains[8:16], axis=0, keepdims=True),
            jnp.zeros((6, C), F32),
        ],
        axis=0,
    )
    for axis, size in (("face", faces), ("rep", reps)):
        small = jnp.broadcast_to(small.astype(BF)[None], (size,) + small.shape)
        small = jnp.sum(swap(small, axis).astype(F32), axis=0)
    small = small * norm_scale
    return (
        result[None],
        grad_input[None],
        small[:56].reshape(7, 8, C)[:, :7],
        small[56],
        small[57],
        grad_win,
        grad_wout,
    )


def solution(mesh):
    return jax.shard_map(
        body,
        mesh=mesh,
        in_specs=(P("rep", "face"), P("rep", "face")) + (P(),) * 9,
        out_specs=(P("rep", "face"), P("rep", "face")) + (P(),) * 5,
        check_vma=False,
    )
```

```python
import functools
import math

import jax
import jax.numpy as jnp
import numpy as np
from jax import lax
from jax.experimental import pallas as pl
from jax.experimental.pallas import tpu as pltpu
from jax.sharding import PartitionSpec as P

BF = jnp.bfloat16
F32 = jnp.float32
N = 32
J = 16
C = 256
HALF = 128
HID = 1024
T = 2
PARTS = 16
KB = 48
SENT = PARTS * KB
LOCAL = 2 * 3 * N
SIDE = 8
MIB = 1024 * 1024


def band_pixel(e, r, p):
    return ((r, p), (p, N - 1 - r), (N - 1 - r, N - 1 - p), (N - 1 - p, r))[e]


def turned_pixel(e, i, j):
    last = N + 5
    return ((i, j), (j, last - i), (last - i, last - j), (last - j, i))[e]


def block_of(e):
    return (0, 1, 0, 2)[e]


def edge_of(t, block):
    return ((0, 1, 3), (2, 1, 3))[t][block]


def chunk_row(t, e, r, p):
    return (p // 2) * KB + block_of(e) * 16 + t * 6 + (p % 2) * 3 + r


def corner_row(t, e, r, c):
    return (r * 3 + c) * KB + t * 16 + 12 + e


def source_pixels():
    pixels = np.full((SENT,), -1, np.int32)
    for t in range(T):
        for e in range(4):
            for r in range(3):
                if e != 2 - 2 * t:
                    for p in range(N):
                        y, x = band_pixel(e, r, p)
                        pixels[chunk_row(t, e, r, p)] = t * N * N + y * N + x
                for c in range(3):
                    y, x = band_pixel(e, r, c)
                    pixels[corner_row(t, e, r, c)] = t * N * N + y * N + x
    return pixels


def rim_sources(t):
    table = {}
    for e in range(4):
        for i in range(3):
            for j in range(N):
                pixel = turned_pixel(e, i, j + 3)
                if e == 2 - 2 * t:
                    y, x = band_pixel((e + 2) % 4, 2 - i, j)
                    y = y if t == 0 else y - (N - 3)
                    row = SENT + t * 3 * N + y * N + x
                    table[pixel] = (e, row, row)
                else:
                    flipped = chunk_row(t, e, 2 - i, N - 1 - j)
                    table[pixel] = (e, chunk_row(t, e, 2 - i, j), flipped)
            for j in range(3):
                pixel = turned_pixel(e, i, j)
                table[pixel] = (
                    4 + e,
                    corner_row(t, e, 2 - i, 2 - j),
                    corner_row(t, e, 2 - j, 2 - i),
                )
    return table


def tables_of(pixels):
    tables = [rim_sources(t) for t in range(T)]
    piece = np.zeros((len(pixels), T * 8), np.int32)
    plain = np.full((len(pixels),), -1, np.int32)
    flipped = np.full((len(pixels),), -1, np.int32)
    for row, (t, p, q) in enumerate(pixels):
        if (p, q) in tables[t]:
            which, plain[row], flipped[row] = tables[t][p, q]
            piece[row, t * 8 + which] = 1
    return piece, plain, flipped


def rows_of(tables, flags):
    piece, plain, flipped = tables
    is_flipped = jnp.sum(piece * flags.reshape(1, -1), axis=1) > 0
    return jnp.where(is_flipped, flipped, plain)


def forward_rim_pixels():
    rows = [(t, p, q + 3) for p in (0, 1, 2, 35, 36, 37) for t in range(T) for q in range(N)]
    for p in range(N + 6):
        for t in range(T):
            rows += [(t, p, q) for q in (0, 1, 2, 35, 36, 37)] + [(t, -9, -9)] * 2
    return rows


RIM_PAIRS = (-2, -1, 16, 17)


def backward_rim_pixels():
    rows = []
    for u in range(2):
        for p in (0, 1, 2, 35, 36, 37):
            rows += [(t, p, 3 + 2 * j + u) for t in range(T) for j in range(J)]
        for k in range(19):
            for v in range(2):
                rows += [(t, 2 * k + v, 3 + 2 * j + u) for t in range(T) for j in RIM_PAIRS]
        rows += [(0, -9, -9)] * 16
    return rows


def pair_selector():
    sel = np.zeros((4, 128, 4 * (N + SIDE)), np.float32)
    for d in range(4):
        for s in range(2):
            for j in range(J):
                q = 2 * (j + d) + s
                for at in range(4):
                    if q < 3:
                        column = 4 * N + at * SIDE + q
                    elif q < N + 3:
                        column = at * N + q - 3
                    else:
                        column = 4 * N + at * SIDE + q - N
                    sel[at, d * 32 + s * 16 + j, column] = 1
    return sel.reshape(512, 4 * (N + SIDE))


def grad_selector():
    sel = np.zeros((768, 3, T, 32), np.float32)
    for d in range(4):
        for s in range(2):
            for j in range(J):
                col = 2 * (j + d) + s - 3
                if 0 <= col < N:
                    for v in range(2):
                        for t in range(T):
                            row = (v * T + t) * 128 + d * 32 + s * 16 + j
                            sel[row, 1 + v, t, (col % 2) * 16 + col // 2] = 1
    rim = grad_rim_selector().reshape(128, 2, T, 32)
    sel[512:640, 1:3] = rim
    sel[640:768, 0:2] = rim
    return sel.reshape(768, 192)


def grad_rim_selector():
    sel = np.zeros((128, 128), np.float32)
    for d in range(4):
        for s in range(2):
            for v in range(2):
                for t in range(T):
                    for at, j in enumerate(RIM_PAIRS):
                        col = 2 * (j + d) + s - 3
                        if 0 <= col < N:
                            row = (d * 2 + s) * 16 + v * 8 + t * 4 + at
                            sel[row, v * 64 + t * 32 + (col % 2) * 16 + col // 2] = 1
    return sel


def split_columns():
    sel = np.zeros((256, 256), np.float32)
    for r in range(8):
        for col in range(N):
            sel[r * 32 + (col % 2) * 16 + col // 2, r * 32 + col] = 1
    return sel


def dot(a, b):
    return jnp.dot(a, b, preferred_element_type=F32)


def fetch(pairs, sems):
    copies = [
        pltpu.make_async_copy(src, dst, sems.at[i]) for i, (src, dst) in enumerate(pairs)
    ]
    for copy in copies:
        copy.start()
    return copies


def pack_kernel(fields_in, pixel_in, out_ref, fields_ref, pixel_ref, sems):
    for copy in fetch([(pixel_in, pixel_ref), (fields_in, fields_ref)], sems):
        copy.wait()
    x = fields_ref[...].reshape(T * N * N, C)
    for m in range(4):
        rows = SENT // 4
        pixel = pixel_ref[m * rows : (m + 1) * rows]
        columns = lax.broadcasted_iota(jnp.int32, (rows, T * N * N), 1)
        pick = jnp.where(columns == pixel, 1.0, 0.0).astype(BF)
        out_ref[m * 4 : (m + 1) * 4] = dot(pick, x).astype(BF).reshape(4, KB, C)


def build_weights(kern_ref, w_ref, mirrored, halves=(0, 1)):
    eye = lax.broadcasted_iota(jnp.int32, (HALF, HALF), 0) == lax.broadcasted_iota(
        jnp.int32, (HALF, HALF), 1
    )
    zero = jnp.zeros((HALF, HALF), BF)

    def step(a, carry):
        row = 6 - a if mirrored else a
        taps = kern_ref[row]
        for at, h in enumerate(halves):
            blocks = [
                jnp.where(eye, taps[b : b + 1, h * HALF : (h + 1) * HALF], 0.0).astype(BF)
                for b in range(7)
            ]
            if mirrored:
                blocks = blocks[::-1]
            for d in range(4):
                for s in range(2):
                    for u in range(2):
                        b = 2 * d + s - u
                        block = blocks[b] if 0 <= b <= 6 else zero
                        top = d * 256 + s * HALF
                        w_ref[at, a, top : top + HALF, u * HALF : (u + 1) * HALF] = block
        return carry

    lax.fori_loop(0, 7, step, 0)


def spread(picked, q_ref, index, base):
    rows = picked.shape[0] // 8
    for d in range(4):
        for s in range(2):
            at = (d * 2 + s) * rows
            for h in range(2):
                lane = d * 256 + s * HALF
                q_ref[h, index, base : base + rows, lane : lane + HALF] = picked[
                    at : at + rows, h * HALF : (h + 1) * HALF
                ]


def forward_kernel(
    fields_in,
    og_in,
    recv_in,
    rim_in,
    kern_ref,
    gain_ref,
    shift_ref,
    win_in,
    wout_in,
    win_t_in,
    wout_t_in,
    psel_in,
    split_in,
    merge_in,
    result_out,
    wide_ref,
    gz_out,
    fields_ref,
    recv_ref,
    rim_ref,
    og_ref,
    win_ref,
    wout_ref,
    win_t_ref,
    wout_t_ref,
    psel_ref,
    split_ref,
    merge_ref,
    result_ref,
    gz_ref,
    mid_ref,
    side_ref,
    q_ref,
    w_ref,
    x_ref,
    o_ref,
    z_ref,
    gwin_ref,
    gwout_ref,
    gains_ref,
    g_ref,
    gt_ref,
    small_ref,
    sems,
):
    copies = fetch(
        [
            (rim_in, rim_ref),
            (recv_in, recv_ref),
            (fields_in, fields_ref),
            (psel_in, psel_ref),
            (og_in, og_ref),
            (split_in, split_ref),
            (win_in, win_ref),
            (wout_in, wout_ref),
            (win_t_in, win_t_ref),
            (wout_t_in, wout_t_ref),
            (merge_in, merge_ref),
        ],
        sems,
    )
    build_weights(kern_ref, w_ref, False)
    for copy in copies[:4]:
        copy.wait()
    source = jnp.concatenate(
        [
            recv_ref[...].reshape(SENT, C),
            fields_ref[1, 0:3].reshape(3 * N, C),
            fields_ref[0, N - 3 :].reshape(3 * N, C),
        ],
        axis=0,
    )
    outer = 6 * T * N
    rims = dot(rim_ref[0:outer], source).astype(BF).reshape(6, T, N, C)
    mid_ref[0:3] = rims[0:3]
    mid_ref[N + 3 :] = rims[3:6]
    side_ref[...] = dot(rim_ref[outer:], source).astype(BF).reshape(N + 6, T * SIDE, C)
    for t in range(T):
        mid_ref[3 : N + 3, t] = fields_ref[t]

    def pairs(i, carry):
        block = jnp.concatenate(
            [
                mid_ref[pl.ds(2 * i, 2)].reshape(4 * N, C),
                side_ref[pl.ds(2 * i, 2)].reshape(4 * SIDE, C),
            ],
            axis=0,
        )
        picked = dot(psel_ref[...], block).astype(BF)
        for v in range(2):
            for t in range(T):
                at = (v * T + t) * 128
                spread(picked[at : at + 128], q_ref, 2 * i + v, t * 16)
        return carry

    lax.fori_loop(0, (N + 6) // 2, pairs, 0)

    copies[4].wait()
    copies[5].wait()

    def order(m, carry):
        for t in range(T):
            rows = pl.ds(m * 8, 8)
            for src, dst in ((fields_ref, x_ref), (og_ref, o_ref)):
                block = src[t, rows].reshape(256, C)
                dst[rows, t * 32 : (t + 1) * 32] = (
                    dot(split_ref[...], block).astype(BF).reshape(8, 32, C)
                )
        return carry

    lax.fori_loop(0, 4, order, 0)

    def conv(m, carry):
        for h in range(2):
            acc = None
            for a in range(7):
                lhs = q_ref[h, pl.ds(m * 8 + a, 8)].reshape(256, 1024)
                part = dot(lhs, w_ref[h, a])
                acc = part if acc is None else acc + part
            acc = acc.reshape(8, T, 16, 256)
            for t in range(T):
                for u in range(2):
                    base = t * 32 + u * 16
                    z_ref[
                        pl.ds(m * 8, 8), base : base + 16, h * HALF : (h + 1) * HALF
                    ] = acc[:, t, :, u * HALF : (u + 1) * HALF]
        return carry

    lax.fori_loop(0, 4, conv, 0)

    for copy in copies[6:]:
        copy.wait()
    gwin_ref[...] = jnp.zeros_like(gwin_ref)
    gwout_ref[...] = jnp.zeros_like(gwout_ref)
    gains_ref[...] = jnp.zeros_like(gains_ref)
    gz_ref[0] = jnp.zeros((64, C), BF)
    gz_ref[N + 1] = jnp.zeros((64, C), BF)
    gain = gain_ref[...]
    shift = shift_ref[...]

    def mlp(m, carry):
        rows = pl.ds(m * 4, 4)
        z = z_ref[rows].reshape(256, C)
        average = jnp.mean(z, axis=1, keepdims=True)
        centered = z - average
        variance = jnp.mean(centered * centered, axis=1, keepdims=True)
        inv_std = lax.rsqrt(variance + 1e-06)
        normed = centered * inv_std
        zn = (normed * gain + shift).astype(BF)
        og = o_ref[rows].reshape(256, C)
        hidden = dot(zn, win_ref[...])
        cdf = 0.5 * (1.0 + lax.erf(hidden * (1.0 / math.sqrt(2.0))))
        pdf = jnp.exp(-0.5 * hidden * hidden) * (1.0 / math.sqrt(2.0 * math.pi))
        act = (hidden * cdf).astype(BF)
        slope = cdf + hidden * pdf
        out = x_ref[rows].reshape(256, C).astype(F32) + dot(act, wout_ref[...])
        x_ref[rows] = out.astype(BF).reshape(4, 64, C)
        grad_hidden = (dot(og, wout_t_ref[...]) * slope).astype(BF)
        gwout_ref[...] += dot(og.T, act)
        gwin_ref[...] += dot(zn.T, grad_hidden)
        grad_normed = dot(grad_hidden, win_t_ref[...])
        gains_ref[0:8] += jnp.sum((grad_normed * normed).reshape(32, 8, C), axis=0)
        gains_ref[8:16] += jnp.sum(grad_normed.reshape(32, 8, C), axis=0)
        scaled = grad_normed * gain
        grad_z = inv_std * (
            scaled
            - jnp.mean(scaled, axis=1, keepdims=True)
            - normed * jnp.mean(scaled * normed, axis=1, keepdims=True)
        )
        grad_z = grad_z.astype(BF).reshape(4, 64, C)
        gz_ref[pl.ds(m * 4 + 1, 4)] = grad_z
        for h in range(2):
            for t in range(T):
                for u in range(2):
                    g_ref[h, rows, t * 16 : (t + 1) * 16, u * HALF : (u + 1) * HALF] = grad_z[
                        :, t * 32 + u * 16 : t * 32 + u * 16 + 16, h * HALF : (h + 1) * HALF
                    ]
        return carry

    lax.fori_loop(0, 8, mlp, 0)

    def unorder(m, carry):
        for t in range(T):
            rows = pl.ds(m * 8, 8)
            block = x_ref[rows, t * 32 : (t + 1) * 32].reshape(256, C)
            result_ref[t, rows] = dot(merge_ref[...], block).astype(BF).reshape(8, 32, C)
        return carry

    lax.fori_loop(0, 4, unorder, 0)
    copies = fetch([(result_ref, result_out), (gz_ref, gz_out)], sems)

    for h in range(2):
        gt_ref[h] = g_ref[h].reshape(1024, 256).T
    eye = lax.broadcasted_iota(jnp.int32, (HALF, HALF), 0) == lax.broadcasted_iota(
        jnp.int32, (HALF, HALF), 1
    )

    def taps(a, carry):
        for h in range(2):
            prod = dot(gt_ref[h], q_ref[h, pl.ds(a, 32)].reshape(1024, 1024))
            sums = [None] * 7
            for d in range(4):
                for s in range(2):
                    for u in range(2):
                        b = 2 * d + s - u
                        if 0 <= b <= 6:
                            lane = d * 256 + s * HALF
                            block = jnp.where(
                                eye, prod[u * HALF : (u + 1) * HALF, lane : lane + HALF], 0.0
                            )
                            sums[b] = block if sums[b] is None else sums[b] + block
            rows = [jnp.sum(block, axis=0, keepdims=True) for block in sums]
            rows.append(jnp.zeros((1, HALF), F32))
            small_ref[a, :, h * HALF : (h + 1) * HALF] = jnp.concatenate(rows, axis=0)
        return carry

    lax.fori_loop(0, 7, taps, 0)
    small_ref[7] = jnp.concatenate(
        [
            jnp.sum(gains_ref[0:8], axis=0, keepdims=True),
            jnp.sum(gains_ref[8:16], axis=0, keepdims=True),
            jnp.zeros((6, C), F32),
        ],
        axis=0,
    )
    half = wide_ref.shape[0] // 2
    wide_ref[:half, 0:256] = gwout_ref[...].T.astype(BF).reshape(half, 256, C)
    wide_ref[half:, 0:256] = gwin_ref[...].T.astype(BF).reshape(half, 256, C)
    blank = jnp.zeros((8, 8, C), F32)
    wide_ref[:, 256:272] = jnp.concatenate([small_ref[...], blank], axis=1).astype(BF)
    for copy in copies:
        copy.wait()


def rims_kernel(
    gz_ref,
    kern_ref,
    row_ref,
    gsel_ref,
    rsel_ref,
    sent_ref,
    near_ref,
    w_ref,
    g_ref,
    r_ref,
    edge_ref,
):
    build_weights(kern_ref, w_ref, True)
    for h in range(2):
        g_ref[h, 0:6] = jnp.zeros((6, 32, 1024), BF)
        g_ref[h, 12:18] = jnp.zeros((6, 32, 1024), BF)
        r_ref[0, h, 0:3] = jnp.zeros((3, 16, 1024), BF)
        r_ref[0, h, 19:22] = jnp.zeros((3, 16, 1024), BF)
        r_ref[1, h, 0:2] = jnp.zeros((2, 16, 1024), BF)
        r_ref[1, h, 19:22] = jnp.zeros((3, 16, 1024), BF)

    def rim_pairs(i, carry):
        block = gz_ref[pl.ds(2 * i, 3)].reshape(192, C)
        picked = dot(gsel_ref[512:], block).astype(BF)
        spread(picked[0:128], r_ref.at[0], 3 + i, 0)
        spread(picked[128:256], r_ref.at[1], 2 + i, 0)
        return carry

    lax.fori_loop(0, 16, rim_pairs, 0)
    last = dot(rsel_ref[...], gz_ref[N : N + 2].reshape(128, C)).astype(BF)
    spread(last, r_ref.at[1], 18, 0)
    for first, row in ((0, 6), (1, 7), (29, 9), (30, 10)):
        picked = dot(gsel_ref[0:512], gz_ref[first : first + 3].reshape(192, C)).astype(BF)
        for v in range(2):
            for t in range(T):
                at = (v * T + t) * 128
                spread(picked[at : at + 128], g_ref, row + v, t * 16)

    for h in range(2):
        acc = None
        for a in range(7):
            k, v = a // 2, a % 2
            lhs = jnp.concatenate(
                [
                    g_ref[h, a : a + 3].reshape(96, 1024),
                    g_ref[h, 9 + a : 12 + a].reshape(96, 1024),
                    r_ref[v, h, k : k + 19].reshape(304, 1024),
                ],
                axis=0,
            )
            part = dot(lhs, w_ref[h, a])
            acc = part if acc is None else acc + part
        edge_ref[h, 0:496] = acc.astype(BF)
        edge_ref[h, 496:512] = jnp.zeros((16, 256), BF)

    edges = jnp.concatenate(
        [
            jnp.concatenate([edge_ref[0, :, 0:HALF], edge_ref[1, :, 0:HALF]], axis=1),
            jnp.concatenate([edge_ref[0, :, HALF:], edge_ref[1, :, HALF:]], axis=1),
        ],
        axis=0,
    )
    rows = SENT + LOCAL
    pick = lax.broadcasted_iota(jnp.int32, (rows, 1024), 0) == row_ref[...]
    back = dot(jnp.where(pick, 1.0, 0.0).astype(BF), edges)
    sent_ref[...] = back[:SENT].astype(BF).reshape(PARTS, KB, C)
    near_ref[...] = back[SENT:].reshape(2, 3, N, C)


def inside_kernel(h, gz_in, kern_ref, gsel_ref, inner_ref, w_ref, g_ref, gz_ref, sems):
    copies = fetch([(gz_in, gz_ref)], sems)
    build_weights(kern_ref, w_ref, True, (h,))
    g_ref[0:3] = jnp.zeros((3, 32, 1024), BF)
    g_ref[35:38] = jnp.zeros((3, 32, 1024), BF)
    copies[0].wait()

    def pairs(i, carry):
        block = gz_ref[pl.ds(2 * i, 3), :, h * HALF : (h + 1) * HALF].reshape(192, HALF)
        picked = dot(gsel_ref[0:512], block).astype(BF)
        for v in range(2):
            for t in range(T):
                for ds in range(8):
                    at = (v * T + t) * 128 + ds * 16
                    rows = slice(t * 16, (t + 1) * 16)
                    lanes = slice(ds * HALF, (ds + 1) * HALF)
                    g_ref[3 + 2 * i + v, rows, lanes] = picked[at : at + 16]
        return carry

    lax.fori_loop(0, 16, pairs, 0)

    def inside(m, carry):
        acc = None
        for a in range(7):
            lhs = g_ref[pl.ds(m * 8 + a, 8)].reshape(256, 1024)
            part = dot(lhs, w_ref[0, a])
            acc = part if acc is None else acc + part
        acc = acc.reshape(8, T, 16, 256)
        for t in range(T):
            for u in range(2):
                inner_ref[t, pl.ds(m * 8, 8), pl.ds(u, 16, stride=2), :] = acc[
                    :, t, :, u * HALF : (u + 1) * HALF
                ]
        return carry

    lax.fori_loop(0, 4, inside, 0)


def join_kernel(sent_ref, wide_ref, out_ref):
    total = wide_ref[0].astype(F32)
    for rep in range(1, wide_ref.shape[0]):
        total = total + wide_ref[rep].astype(F32)
    total = total.astype(BF)
    out_ref[:, 0:KB] = sent_ref[...]
    out_ref[:, KB : KB + 16] = total[0:256].reshape(PARTS, 16, C)
    for part in range(PARTS):
        out_ref[part, KB + 16 :] = total[256:272]


def return_kernel(got_ref, source_ref, out_ref, small_ref):
    pick = lax.broadcasted_iota(jnp.int32, (SENT, SENT), 0) == source_ref[...]
    pick = jnp.where(pick, 1.0, 0.0).astype(BF)
    routed = dot(pick, got_ref[:, 0:KB].reshape(SENT, C)).astype(BF)
    out_ref[:, 0:KB] = routed.reshape(PARTS, KB, C)
    total = got_ref[0, KB:].astype(F32)
    for part in range(1, PARTS):
        total = total + got_ref[part, KB:].astype(F32)
    total = total.astype(BF)
    small_ref[...] = total[16:]
    for part in range(PARTS):
        out_ref[part, KB:] = total[:16]


def spread_kernel(got_ref, small_ref, out_ref):
    wide = got_ref[:, KB : KB + 16].reshape(256, C)
    small = small_ref[...]
    for rep in range(out_ref.shape[0]):
        out_ref[rep, 0:256] = wide
        out_ref[rep, 256:272] = small


def final_kernel(inner0_ref, inner1_ref, near_ref, og_ref, recv_ref, pixel_ref, out_ref):
    recv = recv_ref[:, 0:KB].reshape(SENT, C)
    for t in range(T):
        for m in range(2):
            rows = N * N // 2
            first = (t * 2 + m) * rows
            pick = lax.broadcasted_iota(jnp.int32, (rows, SENT), 0) + first == pixel_ref[...]
            back = dot(jnp.where(pick, 1.0, 0.0).astype(BF), recv).reshape(N // 2, N, C)
            half = slice(m * N // 2, (m + 1) * N // 2)
            inner = jnp.concatenate([inner0_ref[t, half], inner1_ref[t, half]], axis=2)
            total = inner + og_ref[t, half].astype(F32) + back
            if (t, m) == (1, 0):
                total = jnp.concatenate([total[:3] + near_ref[0], total[3:]], axis=0)
            if (t, m) == (0, 1):
                total = jnp.concatenate([total[:-3], total[-3:] + near_ref[1]], axis=0)
            out_ref[t, half] = total.astype(BF)


def unpack_kernel(norm_scale, got_ref, wout_ref, win_ref, taps_ref, gain_ref, shift_ref):
    half = got_ref.shape[0] // 2
    small = got_ref[:, 256:272].astype(F32) * norm_scale
    taps_ref[...] = small[0:7, 0:7]
    gain_ref[...] = small[7, 0:1]
    shift_ref[...] = small[7, 1:2]
    for rep in range(half):
        rows = slice(rep * 256, (rep + 1) * 256)
        wout_ref[rows] = got_ref[rep, 0:256].astype(F32) * norm_scale
        win_ref[:, rows] = (got_ref[half + rep, 0:256].astype(F32) * norm_scale).T


def call(kernel, outs, scratch=(), out_specs=None, in_specs=None, flops=0, vmem=16):
    options = {}
    if flops:
        options["cost_estimate"] = pl.CostEstimate(
            flops=flops, bytes_accessed=10_000_000, transcendentals=0
        )
    if in_specs is not None:
        options["in_specs"] = in_specs
    if out_specs is not None:
        options["out_specs"] = out_specs
    return pl.pallas_call(
        kernel,
        out_shape=outs,
        scratch_shapes=list(scratch),
        compiler_params=pltpu.CompilerParams(vmem_limit_bytes=vmem * MIB),
        **options,
    )


def swap(array, axes):
    return lax.all_to_all(array, axes, 0, 0, tiled=True)


def body(
    fields,
    out_grad,
    kernel,
    ln_gain,
    ln_shift,
    w_in,
    w_out,
    edge_tile,
    edge_code,
    corner_tile,
    corner_code,
):
    x = fields[0]
    og = out_grad[0]
    faces = lax.axis_size("face")
    reps = lax.axis_size("rep")
    devices = faces * reps
    norm_scale = 1.0 / math.sqrt(devices * T * N * N)
    offset = lax.axis_index("face") * T
    vm = pl.BlockSpec(memory_space=pltpu.VMEM)
    hbm = pl.BlockSpec(memory_space=pltpu.HBM)
    shape = jax.ShapeDtypeStruct

    codes = jnp.concatenate([edge_code, corner_code], axis=1) // 4
    flags = lax.dynamic_slice_in_dim(codes, offset, T, 0)
    odd = jnp.arange(edge_tile.shape[0]) % T
    blocks = []
    for block in range(3):
        edge = [edge_of(t, block) for t in range(T)]
        tile = jnp.where(odd == 0, edge_tile[:, edge[0]], edge_tile[:, edge[1]])
        code = jnp.where(odd == 0, edge_code[:, edge[0]], edge_code[:, edge[1]]) % 4
        place = jnp.where(code == 1, 16, jnp.where(code == 3, 32, 0))
        first = tile // T * KB + place + tile % T * 6
        blocks.append((first[:, None] + np.arange(6)).reshape(-1, 12))
    corners = corner_tile // T * KB + corner_tile % T * 16 + 12 + corner_code % 4
    corners = corners.reshape(-1, T, 4)
    none = jnp.full_like(corners[:, 0], -1)
    source = jnp.concatenate(
        [blocks[0], corners[:, 0], blocks[1], corners[:, 1], blocks[2], none], axis=1
    ).reshape(-1)
    pick = (source[:, None] == jnp.arange(SENT, dtype=jnp.int32)).astype(BF)
    rim_rows = rows_of(tables_of(forward_rim_pixels()), flags)
    rim = (rim_rows[:, None] == jnp.arange(SENT + LOCAL, dtype=jnp.int32)).astype(BF)
    edge_rows = rows_of(tables_of(backward_rim_pixels()), flags)
    pixels = source_pixels()

    taps = jnp.pad(kernel.astype(F32), ((0, 0), (0, 1), (0, 0)))

    sent = call(
        pack_kernel,
        shape((PARTS, KB, C), BF),
        scratch=(
            pltpu.VMEM((T, N, N, C), BF),
            pltpu.VMEM((SENT, 1), jnp.int32),
            pltpu.SemaphoreType.DMA((2,)),
        ),
        in_specs=[hbm, hbm],
        out_specs=vm,
        vmem=60,
    )(x, pixels[:, None])
    got = swap(sent, "face")
    routed = dot(pick, got.reshape(-1, C)).astype(BF).reshape(got.shape)
    got = swap(routed, "face")

    split = split_columns()
    result, wide, gz = call(
        forward_kernel,
        (
            shape((T, N, N, C), BF),
            shape((reps, 272, C), BF),
            shape((N + 2, 64, C), BF),
        ),
        scratch=(
            pltpu.VMEM((T, N, N, C), BF),
            pltpu.VMEM((PARTS, KB, C), BF),
            pltpu.VMEM(rim.shape, BF),
            pltpu.VMEM((T, N, N, C), BF),
            pltpu.VMEM((C, HID), BF),
            pltpu.VMEM((HID, C), BF),
            pltpu.VMEM((HID, C), BF),
            pltpu.VMEM((C, HID), BF),
            pltpu.VMEM((512, 4 * (N + SIDE)), BF),
            pltpu.VMEM((256, 256), BF),
            pltpu.VMEM((256, 256), BF),
            pltpu.VMEM((T, N, N, C), BF),
            pltpu.VMEM((N + 2, 64, C), BF),
            pltpu.VMEM((N + 6, T, N, C), BF),
            pltpu.VMEM((N + 6, T * SIDE, C), BF),
            pltpu.VMEM((2, N + 6, 32, 1024), BF),
            pltpu.VMEM((2, 7, 1024, 256), BF),
            pltpu.VMEM((N, 64, C), BF),
            pltpu.VMEM((N, 64, C), BF),
            pltpu.VMEM((N, 64, C), F32),
            pltpu.VMEM((C, HID), F32),
            pltpu.VMEM((C, HID), F32),
            pltpu.VMEM((16, C), F32),
            pltpu.VMEM((2, N, 32, 256), BF),
            pltpu.VMEM((2, 256, 1024), BF),
            pltpu.VMEM((8, 8, C), F32),
            pltpu.SemaphoreType.DMA((11,)),
        ),
        in_specs=[hbm] * 4 + [vm] * 3 + [hbm] * 7,
        out_specs=(hbm, vm, hbm),
        flops=40_000_000_000,
        vmem=60,
    )(
        x,
        og,
        got,
        rim,
        taps,
        ln_gain[None],
        ln_shift[None],
        w_in,
        w_out,
        w_in.T,
        w_out.T,
        pair_selector().astype(BF),
        split.astype(BF),
        split.T.astype(BF),
    )

    wide = swap(wide, "rep")
    gsel = grad_selector().astype(BF)
    sent, near = call(
        rims_kernel,
        (shape((PARTS, KB, C), BF), shape((2, 3, N, C), F32)),
        scratch=(
            pltpu.VMEM((2, 7, 1024, 256), BF),
            pltpu.VMEM((2, 18, 32, 1024), BF),
            pltpu.VMEM((2, 2, 22, 16, 1024), BF),
            pltpu.VMEM((2, 512, 256), BF),
        ),
        flops=12_000_000_000,
        vmem=32,
    )(gz, taps, edge_rows[None], gsel, grad_rim_selector().astype(BF))
    inner = [
        call(
            functools.partial(inside_kernel, h),
            shape((T, N, N, HALF), F32),
            scratch=(
                pltpu.VMEM((1, 7, 1024, 256), BF),
                pltpu.VMEM((N + 6, 32, 1024), BF),
                pltpu.VMEM((N + 2, 64, C), BF),
                pltpu.SemaphoreType.DMA((1,)),
            ),
            in_specs=[hbm, vm, vm],
            out_specs=vm,
            flops=9_000_000_000,
            vmem=20,
        )(gz, taps, gsel)
        for h in range(2)
    ]
    sent = call(join_kernel, shape((PARTS, KB + 32, C), BF))(sent, wide)
    got = swap(sent, "face")
    routed, small = call(
        return_kernel, (shape((PARTS, KB + 16, C), BF), shape((16, C), BF))
    )(got, source[None])
    got = swap(routed, "face")
    wide = call(spread_kernel, shape((reps, 272, C), BF))(got, small)
    wide = swap(wide, "rep")
    grad_input = call(final_kernel, shape((T, N, N, C), BF), flops=5_000_000_000)(
        *inner, near, og, got, pixels[None]
    )
    grad_wout, grad_win, grad_taps, grad_gain, grad_shift = call(
        functools.partial(unpack_kernel, norm_scale),
        (
            shape((HID, C), F32),
            shape((C, HID), F32),
            shape(kernel.shape, F32),
            shape((1, C), F32),
            shape((1, C), F32),
        ),
    )(wide)
    return (
        result[None],
        grad_input[None],
        grad_taps,
        grad_gain[0],
        grad_shift[0],
        grad_win,
        grad_wout,
    )


def solution(mesh):
    return jax.shard_map(
        body,
        mesh=mesh,
        in_specs=(P("rep", "face"), P("rep", "face")) + (P(),) * 9,
        out_specs=(P("rep", "face"), P("rep", "face")) + (P(),) * 5,
        check_vma=False,
    )
```

```python
import functools
import math

import jax
import jax.numpy as jnp
import numpy as np
from jax import lax
from jax.experimental import pallas as pl
from jax.experimental.pallas import tpu as pltpu
from jax.sharding import PartitionSpec as P

BF = jnp.bfloat16
F32 = jnp.float32
N = 32
J = 16
C = 256
HALF = 128
HID = 1024
T = 2
PARTS = 16
KB = 48
SENT = PARTS * KB
LOCAL = 2 * 3 * N
SIDE = 8
MIB = 1024 * 1024


def band_pixel(e, r, p):
    return ((r, p), (p, N - 1 - r), (N - 1 - r, N - 1 - p), (N - 1 - p, r))[e]


def turned_pixel(e, i, j):
    last = N + 5
    return ((i, j), (j, last - i), (last - i, last - j), (last - j, i))[e]


def block_of(e):
    return (0, 1, 0, 2)[e]


def edge_of(t, block):
    return ((0, 1, 3), (2, 1, 3))[t][block]


def chunk_row(t, e, r, p):
    return (p // 2) * KB + block_of(e) * 16 + t * 6 + (p % 2) * 3 + r


def corner_row(t, e, r, c):
    return (r * 3 + c) * KB + t * 16 + 12 + e


def source_pixels():
    pixels = np.full((SENT,), -1, np.int32)
    for t in range(T):
        for e in range(4):
            for r in range(3):
                if e != 2 - 2 * t:
                    for p in range(N):
                        y, x = band_pixel(e, r, p)
                        pixels[chunk_row(t, e, r, p)] = t * N * N + y * N + x
                for c in range(3):
                    y, x = band_pixel(e, r, c)
                    pixels[corner_row(t, e, r, c)] = t * N * N + y * N + x
    return pixels


def rim_sources(t):
    table = {}
    for e in range(4):
        for i in range(3):
            for j in range(N):
                pixel = turned_pixel(e, i, j + 3)
                if e == 2 - 2 * t:
                    y, x = band_pixel((e + 2) % 4, 2 - i, j)
                    y = y if t == 0 else y - (N - 3)
                    row = SENT + t * 3 * N + y * N + x
                    table[pixel] = (e, row, row)
                else:
                    flipped = chunk_row(t, e, 2 - i, N - 1 - j)
                    table[pixel] = (e, chunk_row(t, e, 2 - i, j), flipped)
            for j in range(3):
                pixel = turned_pixel(e, i, j)
                table[pixel] = (
                    4 + e,
                    corner_row(t, e, 2 - i, 2 - j),
                    corner_row(t, e, 2 - j, 2 - i),
                )
    return table


def tables_of(pixels):
    tables = [rim_sources(t) for t in range(T)]
    piece = np.zeros((len(pixels), T * 8), np.int32)
    plain = np.full((len(pixels),), -1, np.int32)
    flipped = np.full((len(pixels),), -1, np.int32)
    for row, (t, p, q) in enumerate(pixels):
        if (p, q) in tables[t]:
            which, plain[row], flipped[row] = tables[t][p, q]
            piece[row, t * 8 + which] = 1
    return piece, plain, flipped


def rows_of(tables, flags):
    piece, plain, flipped = tables
    is_flipped = jnp.sum(piece * flags.reshape(1, -1), axis=1) > 0
    return jnp.where(is_flipped, flipped, plain)


def forward_rim_pixels():
    rows = [(t, p, q + 3) for p in (0, 1, 2, 35, 36, 37) for t in range(T) for q in range(N)]
    for p in range(N + 6):
        for t in range(T):
            rows += [(t, p, q) for q in (0, 1, 2, 35, 36, 37)] + [(t, -9, -9)] * 2
    return rows


RIM_PAIRS = (-2, -1, 16, 17)


def backward_rim_pixels():
    rows = []
    for u in range(2):
        for p in (0, 1, 2, 35, 36, 37):
            rows += [(t, p, 3 + 2 * j + u) for t in range(T) for j in range(J)]
        for k in range(19):
            for v in range(2):
                rows += [(t, 2 * k + v, 3 + 2 * j + u) for t in range(T) for j in RIM_PAIRS]
        rows += [(0, -9, -9)] * 16
    return rows


def pair_selector():
    sel = np.zeros((4, 128, 4 * (N + SIDE)), np.float32)
    for d in range(4):
        for s in range(2):
            for j in range(J):
                q = 2 * (j + d) + s
                for at in range(4):
                    if q < 3:
                        column = 4 * N + at * SIDE + q
                    elif q < N + 3:
                        column = at * N + q - 3
                    else:
                        column = 4 * N + at * SIDE + q - N
                    sel[at, d * 32 + s * 16 + j, column] = 1
    return sel.reshape(512, 4 * (N + SIDE))


def grad_selector():
    sel = np.zeros((768, 3, T, 32), np.float32)
    for d in range(4):
        for s in range(2):
            for j in range(J):
                col = 2 * (j + d) + s - 3
                if 0 <= col < N:
                    for v in range(2):
                        for t in range(T):
                            row = (v * T + t) * 128 + d * 32 + s * 16 + j
                            sel[row, 1 + v, t, (col % 2) * 16 + col // 2] = 1
    rim = grad_rim_selector().reshape(128, 2, T, 32)
    sel[512:640, 1:3] = rim
    sel[640:768, 0:2] = rim
    return sel.reshape(768, 192)


def grad_rim_selector():
    sel = np.zeros((128, 128), np.float32)
    for d in range(4):
        for s in range(2):
            for v in range(2):
                for t in range(T):
                    for at, j in enumerate(RIM_PAIRS):
                        col = 2 * (j + d) + s - 3
                        if 0 <= col < N:
                            row = (d * 2 + s) * 16 + v * 8 + t * 4 + at
                            sel[row, v * 64 + t * 32 + (col % 2) * 16 + col // 2] = 1
    return sel


def split_columns():
    sel = np.zeros((256, 256), np.float32)
    for r in range(8):
        for col in range(N):
            sel[r * 32 + (col % 2) * 16 + col // 2, r * 32 + col] = 1
    return sel


def dot(a, b):
    return jnp.dot(a, b, preferred_element_type=F32)


def fetch(pairs, sems):
    copies = [
        pltpu.make_async_copy(src, dst, sems.at[i]) for i, (src, dst) in enumerate(pairs)
    ]
    for copy in copies:
        copy.start()
    return copies


def pack_kernel(fields_in, pixel_in, out_ref, fields_ref, pixel_ref, sems):
    for copy in fetch([(pixel_in, pixel_ref), (fields_in, fields_ref)], sems):
        copy.wait()
    x = fields_ref[...].reshape(T * N * N, C)
    for m in range(4):
        rows = SENT // 4
        pixel = pixel_ref[m * rows : (m + 1) * rows]
        columns = lax.broadcasted_iota(jnp.int32, (rows, T * N * N), 1)
        pick = jnp.where(columns == pixel, 1.0, 0.0).astype(BF)
        out_ref[m * 4 : (m + 1) * 4] = dot(pick, x).astype(BF).reshape(4, KB, C)


def build_weights(kern_ref, w_ref, mirrored, halves=(0, 1)):
    eye = lax.broadcasted_iota(jnp.int32, (HALF, HALF), 0) == lax.broadcasted_iota(
        jnp.int32, (HALF, HALF), 1
    )
    zero = jnp.zeros((HALF, HALF), BF)

    def step(a, carry):
        row = 6 - a if mirrored else a
        taps = kern_ref[row]
        for at, h in enumerate(halves):
            blocks = [
                jnp.where(eye, taps[b : b + 1, h * HALF : (h + 1) * HALF], 0.0).astype(BF)
                for b in range(7)
            ]
            if mirrored:
                blocks = blocks[::-1]
            for d in range(4):
                for s in range(2):
                    for u in range(2):
                        b = 2 * d + s - u
                        block = blocks[b] if 0 <= b <= 6 else zero
                        top = d * 256 + s * HALF
                        w_ref[at, a, top : top + HALF, u * HALF : (u + 1) * HALF] = block
        return carry

    lax.fori_loop(0, 7, step, 0)


def spread(picked, q_ref, index, base):
    rows = picked.shape[0] // 8
    for d in range(4):
        for s in range(2):
            at = (d * 2 + s) * rows
            for h in range(2):
                lane = d * 256 + s * HALF
                q_ref[h, index, base : base + rows, lane : lane + HALF] = picked[
                    at : at + rows, h * HALF : (h + 1) * HALF
                ]


def forward_kernel(
    fields_in,
    og_in,
    recv_in,
    row_ref,
    kern_ref,
    gain_ref,
    shift_ref,
    win_in,
    wout_in,
    win_t_in,
    wout_t_in,
    psel_in,
    split_in,
    merge_in,
    result_out,
    wide_ref,
    gz_out,
    fields_ref,
    recv_ref,
    og_ref,
    win_ref,
    wout_ref,
    win_t_ref,
    wout_t_ref,
    psel_ref,
    split_ref,
    merge_ref,
    result_ref,
    gz_ref,
    mid_ref,
    side_ref,
    q_ref,
    w_ref,
    x_ref,
    o_ref,
    z_ref,
    gwin_ref,
    gwout_ref,
    gains_ref,
    g_ref,
    gt_ref,
    small_ref,
    sems,
):
    copies = fetch(
        [
            (recv_in, recv_ref),
            (fields_in, fields_ref),
            (psel_in, psel_ref),
        ],
        sems,
    )
    build_weights(kern_ref, w_ref, False)
    for copy in copies:
        copy.wait()
    copies = fetch(
        [
            (og_in, og_ref),
            (split_in, split_ref),
            (win_in, win_ref),
            (wout_in, wout_ref),
            (win_t_in, win_t_ref),
            (wout_t_in, wout_t_ref),
            (merge_in, merge_ref),
        ],
        sems,
    )
    source = jnp.concatenate(
        [
            recv_ref[...].reshape(SENT, C),
            fields_ref[1, 0:3].reshape(3 * N, C),
            fields_ref[0, N - 3 :].reshape(3 * N, C),
        ],
        axis=0,
    )
    outer = 6 * T * N
    row = jnp.broadcast_to(row_ref[...], (8, row_ref.shape[1])).T[:, 0:1]
    columns = lax.broadcasted_iota(jnp.int32, (row.shape[0], SENT + LOCAL), 1)
    pick = jnp.where(columns == row, 1.0, 0.0).astype(BF)
    rims = dot(pick, source)
    rims, sides = rims[:outer].astype(BF).reshape(6, T, N, C), rims[outer:]
    mid_ref[0:3] = rims[0:3]
    mid_ref[N + 3 :] = rims[3:6]
    side_ref[...] = sides.astype(BF).reshape(N + 6, T * SIDE, C)
    for t in range(T):
        mid_ref[3 : N + 3, t] = fields_ref[t]

    def pairs(i, carry):
        block = jnp.concatenate(
            [
                mid_ref[pl.ds(2 * i, 2)].reshape(4 * N, C),
                side_ref[pl.ds(2 * i, 2)].reshape(4 * SIDE, C),
            ],
            axis=0,
        )
        picked = dot(psel_ref[...], block).astype(BF)
        for v in range(2):
            for t in range(T):
                at = (v * T + t) * 128
                spread(picked[at : at + 128], q_ref, 2 * i + v, t * 16)
        return carry

    for i in range((N + 6) // 2):
        pairs(i, 0)

    copies[0].wait()
    copies[1].wait()

    def order(m, carry):
        for t in range(T):
            rows = pl.ds(m * 8, 8)
            for src, dst in ((fields_ref, x_ref), (og_ref, o_ref)):
                block = src[t, rows].reshape(256, C)
                dst[rows, t * 32 : (t + 1) * 32] = (
                    dot(split_ref[...], block).astype(BF).reshape(8, 32, C)
                )
        return carry

    for m in range(4):
        order(m, 0)

    def conv(m, carry):
        for h in range(2):
            acc = None
            for a in range(7):
                lhs = q_ref[h, pl.ds(m * 8 + a, 8)].reshape(256, 1024)
                part = dot(lhs, w_ref[h, a])
                acc = part if acc is None else acc + part
            acc = acc.reshape(8, T, 16, 256)
            for t in range(T):
                for u in range(2):
                    base = t * 32 + u * 16
                    z_ref[
                        pl.ds(m * 8, 8), base : base + 16, h * HALF : (h + 1) * HALF
                    ] = acc[:, t, :, u * HALF : (u + 1) * HALF]
        return carry

    lax.fori_loop(0, 4, conv, 0)

    for copy in copies[2:]:
        copy.wait()
    gwin_ref[...] = jnp.zeros_like(gwin_ref)
    gwout_ref[...] = jnp.zeros_like(gwout_ref)
    gains_ref[...] = jnp.zeros_like(gains_ref)
    gz_ref[0] = jnp.zeros((64, C), BF)
    gz_ref[N + 1] = jnp.zeros((64, C), BF)
    gain = gain_ref[...]
    shift = shift_ref[...]

    def mlp(m, carry):
        rows = pl.ds(m * 8, 8)
        z = z_ref[rows].reshape(512, C)
        average = jnp.mean(z, axis=1, keepdims=True)
        centered = z - average
        variance = jnp.mean(centered * centered, axis=1, keepdims=True)
        inv_std = lax.rsqrt(variance + 1e-06)
        normed = centered * inv_std
        zn = (normed * gain + shift).astype(BF)
        og = o_ref[rows].reshape(512, C)
        hidden = dot(zn, win_ref[...])
        cdf = 0.5 * (1.0 + lax.erf(hidden * (1.0 / math.sqrt(2.0))))
        pdf = jnp.exp(-0.5 * hidden * hidden) * (1.0 / math.sqrt(2.0 * math.pi))
        act = (hidden * cdf).astype(BF)
        slope = cdf + hidden * pdf
        out = x_ref[rows].reshape(512, C).astype(F32) + dot(act, wout_ref[...])
        x_ref[rows] = out.astype(BF).reshape(8, 64, C)
        grad_hidden = (dot(og, wout_t_ref[...]) * slope).astype(BF)
        gwout_ref[...] += dot(og.T, act)
        gwin_ref[...] += dot(zn.T, grad_hidden)
        grad_normed = dot(grad_hidden, win_t_ref[...])
        gains_ref[0:8] += jnp.sum((grad_normed * normed).reshape(64, 8, C), axis=0)
        gains_ref[8:16] += jnp.sum(grad_normed.reshape(64, 8, C), axis=0)
        scaled = grad_normed * gain
        grad_z = inv_std * (
            scaled
            - jnp.mean(scaled, axis=1, keepdims=True)
            - normed * jnp.mean(scaled * normed, axis=1, keepdims=True)
        )
        grad_z = grad_z.astype(BF).reshape(8, 64, C)
        gz_ref[pl.ds(m * 8 + 1, 8)] = grad_z
        for h in range(2):
            for t in range(T):
                for u in range(2):
                    g_ref[h, rows, t * 16 : (t + 1) * 16, u * HALF : (u + 1) * HALF] = grad_z[
                        :, t * 32 + u * 16 : t * 32 + u * 16 + 16, h * HALF : (h + 1) * HALF
                    ]
        return carry

    for m in range(4):
        mlp(m, 0)

    def unorder(m, carry):
        for t in range(T):
            rows = pl.ds(m * 8, 8)
            block = x_ref[rows, t * 32 : (t + 1) * 32].reshape(256, C)
            result_ref[t, rows] = dot(merge_ref[...], block).astype(BF).reshape(8, 32, C)
        return carry

    for m in range(4):
        unorder(m, 0)
    copies = fetch([(result_ref, result_out), (gz_ref, gz_out)], sems)

    for h in range(2):
        gt_ref[h] = g_ref[h].reshape(1024, 256).T
    eye = lax.broadcasted_iota(jnp.int32, (HALF, HALF), 0) == lax.broadcasted_iota(
        jnp.int32, (HALF, HALF), 1
    )

    def taps(a, carry):
        for h in range(2):
            prod = dot(gt_ref[h], q_ref[h, pl.ds(a, 32)].reshape(1024, 1024))
            sums = [None] * 7
            for d in range(4):
                for s in range(2):
                    for u in range(2):
                        b = 2 * d + s - u
                        if 0 <= b <= 6:
                            lane = d * 256 + s * HALF
                            block = jnp.where(
                                eye, prod[u * HALF : (u + 1) * HALF, lane : lane + HALF], 0.0
                            )
                            sums[b] = block if sums[b] is None else sums[b] + block
            rows = [jnp.sum(block, axis=0, keepdims=True) for block in sums]
            rows.append(jnp.zeros((1, HALF), F32))
            small_ref[a, :, h * HALF : (h + 1) * HALF] = jnp.concatenate(rows, axis=0)
        return carry

    for a in range(7):
        taps(a, 0)
    small_ref[7] = jnp.concatenate(
        [
            jnp.sum(gains_ref[0:8], axis=0, keepdims=True),
            jnp.sum(gains_ref[8:16], axis=0, keepdims=True),
            jnp.zeros((6, C), F32),
        ],
        axis=0,
    )
    half = wide_ref.shape[0] // 2
    wide_ref[:half, 0:256] = gwout_ref[...].T.astype(BF).reshape(half, 256, C)
    wide_ref[half:, 0:256] = gwin_ref[...].T.astype(BF).reshape(half, 256, C)
    blank = jnp.zeros((8, 8, C), F32)
    wide_ref[:, 256:272] = jnp.concatenate([small_ref[...], blank], axis=1).astype(BF)
    for copy in copies:
        copy.wait()


def rims_kernel(
    gz_ref,
    kern_ref,
    row_ref,
    gsel_ref,
    rsel_ref,
    sent_ref,
    near_ref,
    w_ref,
    g_ref,
    r_ref,
    edge_ref,
):
    build_weights(kern_ref, w_ref, True)
    for h in range(2):
        g_ref[h, 0:6] = jnp.zeros((6, 32, 1024), BF)
        g_ref[h, 12:18] = jnp.zeros((6, 32, 1024), BF)
        r_ref[0, h, 0:3] = jnp.zeros((3, 16, 1024), BF)
        r_ref[0, h, 19:22] = jnp.zeros((3, 16, 1024), BF)
        r_ref[1, h, 0:2] = jnp.zeros((2, 16, 1024), BF)
        r_ref[1, h, 19:22] = jnp.zeros((3, 16, 1024), BF)

    def rim_pairs(i, carry):
        block = gz_ref[pl.ds(2 * i, 3)].reshape(192, C)
        picked = dot(gsel_ref[512:], block).astype(BF)
        spread(picked[0:128], r_ref.at[0], 3 + i, 0)
        spread(picked[128:256], r_ref.at[1], 2 + i, 0)
        return carry

    for i in range(16):
        rim_pairs(i, 0)
    last = dot(rsel_ref[...], gz_ref[N : N + 2].reshape(128, C)).astype(BF)
    spread(last, r_ref.at[1], 18, 0)
    for first, row in ((0, 6), (1, 7), (29, 9), (30, 10)):
        picked = dot(gsel_ref[0:512], gz_ref[first : first + 3].reshape(192, C)).astype(BF)
        for v in range(2):
            for t in range(T):
                at = (v * T + t) * 128
                spread(picked[at : at + 128], g_ref, row + v, t * 16)

    for h in range(2):
        acc = None
        for a in range(7):
            k, v = a // 2, a % 2
            lhs = jnp.concatenate(
                [
                    g_ref[h, a : a + 3].reshape(96, 1024),
                    g_ref[h, 9 + a : 12 + a].reshape(96, 1024),
                    r_ref[v, h, k : k + 19].reshape(304, 1024),
                ],
                axis=0,
            )
            part = dot(lhs, w_ref[h, a])
            acc = part if acc is None else acc + part
        edge_ref[h, 0:496] = acc.astype(BF)
        edge_ref[h, 496:512] = jnp.zeros((16, 256), BF)

    edges = jnp.concatenate(
        [
            jnp.concatenate([edge_ref[0, :, 0:HALF], edge_ref[1, :, 0:HALF]], axis=1),
            jnp.concatenate([edge_ref[0, :, HALF:], edge_ref[1, :, HALF:]], axis=1),
        ],
        axis=0,
    )
    rows = SENT + LOCAL
    pick = lax.broadcasted_iota(jnp.int32, (rows, 1024), 0) == row_ref[...]
    back = dot(jnp.where(pick, 1.0, 0.0).astype(BF), edges)
    sent_ref[...] = back[:SENT].astype(BF).reshape(PARTS, KB, C)
    near_ref[...] = back[SENT:].reshape(2, 3, N, C)


def inside_kernel(h, gz_in, kern_ref, gsel_ref, inner_ref, w_ref, g_ref, gz_ref, sems):
    copies = fetch([(gz_in, gz_ref)], sems)
    build_weights(kern_ref, w_ref, True, (h,))
    g_ref[0:3] = jnp.zeros((3, 32, 1024), BF)
    g_ref[35:38] = jnp.zeros((3, 32, 1024), BF)
    copies[0].wait()

    def pairs(i, carry):
        block = gz_ref[pl.ds(2 * i, 3), :, h * HALF : (h + 1) * HALF].reshape(192, HALF)
        picked = dot(gsel_ref[0:512], block).astype(BF)
        for v in range(2):
            for t in range(T):
                for ds in range(8):
                    at = (v * T + t) * 128 + ds * 16
                    rows = slice(t * 16, (t + 1) * 16)
                    lanes = slice(ds * HALF, (ds + 1) * HALF)
                    g_ref[3 + 2 * i + v, rows, lanes] = picked[at : at + 16]
        return carry

    for i in range(16):
        pairs(i, 0)

    def inside(m, carry):
        acc = None
        for a in range(7):
            lhs = g_ref[pl.ds(m * 8 + a, 8)].reshape(256, 1024)
            part = dot(lhs, w_ref[0, a])
            acc = part if acc is None else acc + part
        acc = acc.reshape(8, T, 16, 256)
        for t in range(T):
            for u in range(2):
                inner_ref[t, pl.ds(m * 8, 8), pl.ds(u, 16, stride=2), :] = acc[
                    :, t, :, u * HALF : (u + 1) * HALF
                ]
        return carry

    lax.fori_loop(0, 4, inside, 0)


def join_kernel(sent_ref, wide_ref, out_ref):
    total = wide_ref[0].astype(F32)
    for rep in range(1, wide_ref.shape[0]):
        total = total + wide_ref[rep].astype(F32)
    total = total.astype(BF)
    out_ref[:, 0:KB] = sent_ref[...]
    out_ref[:, KB : KB + 16] = total[0:256].reshape(PARTS, 16, C)
    for part in range(PARTS):
        out_ref[part, KB + 16 :] = total[256:272]


def return_kernel(got_ref, source_ref, out_ref, small_ref):
    pick = lax.broadcasted_iota(jnp.int32, (SENT, SENT), 0) == source_ref[...]
    pick = jnp.where(pick, 1.0, 0.0).astype(BF)
    routed = dot(pick, got_ref[:, 0:KB].reshape(SENT, C)).astype(BF)
    out_ref[:, 0:KB] = routed.reshape(PARTS, KB, C)
    total = got_ref[0, KB:].astype(F32)
    for part in range(1, PARTS):
        total = total + got_ref[part, KB:].astype(F32)
    total = total.astype(BF)
    small_ref[...] = total[16:]
    for part in range(PARTS):
        out_ref[part, KB:] = total[:16]


def spread_kernel(got_ref, small_ref, out_ref):
    wide = got_ref[:, KB : KB + 16].reshape(256, C)
    small = small_ref[...]
    for rep in range(out_ref.shape[0]):
        out_ref[rep, 0:256] = wide
        out_ref[rep, 256:272] = small


def final_kernel(inner0_ref, inner1_ref, near_ref, og_ref, recv_ref, pixel_ref, out_ref):
    recv = recv_ref[:, 0:KB].reshape(SENT, C)
    for t in range(T):
        for m in range(2):
            rows = N * N // 2
            first = (t * 2 + m) * rows
            pick = lax.broadcasted_iota(jnp.int32, (rows, SENT), 0) + first == pixel_ref[...]
            back = dot(jnp.where(pick, 1.0, 0.0).astype(BF), recv).reshape(N // 2, N, C)
            half = slice(m * N // 2, (m + 1) * N // 2)
            inner = jnp.concatenate([inner0_ref[t, half], inner1_ref[t, half]], axis=2)
            total = inner + og_ref[t, half].astype(F32) + back
            if (t, m) == (1, 0):
                total = jnp.concatenate([total[:3] + near_ref[0], total[3:]], axis=0)
            if (t, m) == (0, 1):
                total = jnp.concatenate([total[:-3], total[-3:] + near_ref[1]], axis=0)
            out_ref[t, half] = total.astype(BF)


def unpack_kernel(norm_scale, got_ref, wout_ref, win_ref, taps_ref, gain_ref, shift_ref):
    half = got_ref.shape[0] // 2
    small = got_ref[:, 256:272].astype(F32) * norm_scale
    taps_ref[...] = small[0:7, 0:7]
    gain_ref[...] = small[7, 0:1]
    shift_ref[...] = small[7, 1:2]
    for rep in range(half):
        rows = slice(rep * 256, (rep + 1) * 256)
        wout_ref[rows] = got_ref[rep, 0:256].astype(F32) * norm_scale
        win_ref[:, rows] = (got_ref[half + rep, 0:256].astype(F32) * norm_scale).T


def call(kernel, outs, scratch=(), out_specs=None, in_specs=None, flops=0, vmem=16):
    options = {}
    if flops:
        options["cost_estimate"] = pl.CostEstimate(
            flops=flops, bytes_accessed=10_000_000, transcendentals=0
        )
    if in_specs is not None:
        options["in_specs"] = in_specs
    if out_specs is not None:
        options["out_specs"] = out_specs
    return pl.pallas_call(
        kernel,
        out_shape=outs,
        scratch_shapes=list(scratch),
        compiler_params=pltpu.CompilerParams(vmem_limit_bytes=vmem * MIB),
        **options,
    )


def swap(array, axes):
    return lax.all_to_all(array, axes, 0, 0, tiled=True)


def body(
    fields,
    out_grad,
    kernel,
    ln_gain,
    ln_shift,
    w_in,
    w_out,
    edge_tile,
    edge_code,
    corner_tile,
    corner_code,
):
    x = fields[0]
    og = out_grad[0]
    faces = lax.axis_size("face")
    reps = lax.axis_size("rep")
    devices = faces * reps
    norm_scale = 1.0 / math.sqrt(devices * T * N * N)
    offset = lax.axis_index("face") * T
    vm = pl.BlockSpec(memory_space=pltpu.VMEM)
    hbm = pl.BlockSpec(memory_space=pltpu.HBM)
    shape = jax.ShapeDtypeStruct

    codes = jnp.concatenate([edge_code, corner_code], axis=1) // 4
    flags = lax.dynamic_slice_in_dim(codes, offset, T, 0)
    odd = jnp.arange(edge_tile.shape[0]) % T
    blocks = []
    for block in range(3):
        edge = [edge_of(t, block) for t in range(T)]
        tile = jnp.where(odd == 0, edge_tile[:, edge[0]], edge_tile[:, edge[1]])
        code = jnp.where(odd == 0, edge_code[:, edge[0]], edge_code[:, edge[1]]) % 4
        place = jnp.where(code == 1, 16, jnp.where(code == 3, 32, 0))
        first = tile // T * KB + place + tile % T * 6
        blocks.append((first[:, None] + np.arange(6)).reshape(-1, 12))
    corners = corner_tile // T * KB + corner_tile % T * 16 + 12 + corner_code % 4
    corners = corners.reshape(-1, T, 4)
    none = jnp.full_like(corners[:, 0], -1)
    source = jnp.concatenate(
        [blocks[0], corners[:, 0], blocks[1], corners[:, 1], blocks[2], none], axis=1
    ).reshape(-1)
    pick = (source[:, None] == jnp.arange(SENT, dtype=jnp.int32)).astype(BF)
    rim_rows = rows_of(tables_of(forward_rim_pixels()), flags)
    edge_rows = rows_of(tables_of(backward_rim_pixels()), flags)
    pixels = source_pixels()

    taps = jnp.pad(kernel.astype(F32), ((0, 0), (0, 1), (0, 0)))

    sent = call(
        pack_kernel,
        shape((PARTS, KB, C), BF),
        scratch=(
            pltpu.VMEM((T, N, N, C), BF),
            pltpu.VMEM((SENT, 1), jnp.int32),
            pltpu.SemaphoreType.DMA((2,)),
        ),
        in_specs=[hbm, hbm],
        out_specs=vm,
        vmem=60,
    )(x, pixels[:, None])
    got = swap(sent, "face")
    routed = dot(pick, got.reshape(-1, C)).astype(BF).reshape(got.shape)
    got = swap(routed, "face")

    split = split_columns()
    result, wide, gz = call(
        forward_kernel,
        (
            shape((T, N, N, C), BF),
            shape((reps, 272, C), BF),
            shape((N + 2, 64, C), BF),
        ),
        scratch=(
            pltpu.VMEM((T, N, N, C), BF),
            pltpu.VMEM((PARTS, KB, C), BF),
            pltpu.VMEM((T, N, N, C), BF),
            pltpu.VMEM((C, HID), BF),
            pltpu.VMEM((HID, C), BF),
            pltpu.VMEM((HID, C), BF),
            pltpu.VMEM((C, HID), BF),
            pltpu.VMEM((512, 4 * (N + SIDE)), BF),
            pltpu.VMEM((256, 256), BF),
            pltpu.VMEM((256, 256), BF),
            pltpu.VMEM((T, N, N, C), BF),
            pltpu.VMEM((N + 2, 64, C), BF),
            pltpu.VMEM((N + 6, T, N, C), BF),
            pltpu.VMEM((N + 6, T * SIDE, C), BF),
            pltpu.VMEM((2, N + 6, 32, 1024), BF),
            pltpu.VMEM((2, 7, 1024, 256), BF),
            pltpu.VMEM((N, 64, C), BF),
            pltpu.VMEM((N, 64, C), BF),
            pltpu.VMEM((N, 64, C), F32),
            pltpu.VMEM((C, HID), F32),
            pltpu.VMEM((C, HID), F32),
            pltpu.VMEM((16, C), F32),
            pltpu.VMEM((2, N, 32, 256), BF),
            pltpu.VMEM((2, 256, 1024), BF),
            pltpu.VMEM((8, 8, C), F32),
            pltpu.SemaphoreType.DMA((7,)),
        ),
        in_specs=[hbm] * 3 + [vm] * 4 + [hbm] * 7,
        out_specs=(hbm, vm, hbm),
        flops=40_000_000_000,
        vmem=60,
    )(
        x,
        og,
        got,
        rim_rows[None],
        taps,
        ln_gain[None],
        ln_shift[None],
        w_in,
        w_out,
        w_in.T,
        w_out.T,
        pair_selector().astype(BF),
        split.astype(BF),
        split.T.astype(BF),
    )

    wide = swap(wide, "rep")
    gsel = grad_selector().astype(BF)
    sent, near = call(
        rims_kernel,
        (shape((PARTS, KB, C), BF), shape((2, 3, N, C), F32)),
        scratch=(
            pltpu.VMEM((2, 7, 1024, 256), BF),
            pltpu.VMEM((2, 18, 32, 1024), BF),
            pltpu.VMEM((2, 2, 22, 16, 1024), BF),
            pltpu.VMEM((2, 512, 256), BF),
        ),
        flops=12_000_000_000,
        vmem=32,
    )(gz, taps, edge_rows[None], gsel, grad_rim_selector().astype(BF))
    inner = [
        call(
            functools.partial(inside_kernel, h),
            shape((T, N, N, HALF), F32),
            scratch=(
                pltpu.VMEM((1, 7, 1024, 256), BF),
                pltpu.VMEM((N + 6, 32, 1024), BF),
                pltpu.VMEM((N + 2, 64, C), BF),
                pltpu.SemaphoreType.DMA((1,)),
            ),
            in_specs=[hbm, vm, vm],
            out_specs=vm,
            flops=9_000_000_000,
            vmem=20,
        )(gz, taps, gsel)
        for h in range(2)
    ]
    sent = call(join_kernel, shape((PARTS, KB + 32, C), BF))(sent, wide)
    got = swap(sent, "face")
    routed, small = call(
        return_kernel, (shape((PARTS, KB + 16, C), BF), shape((16, C), BF))
    )(got, source[None])
    got = swap(routed, "face")
    wide = call(spread_kernel, shape((reps, 272, C), BF))(got, small)
    wide = swap(wide, "rep")
    grad_input = call(final_kernel, shape((T, N, N, C), BF), flops=5_000_000_000)(
        *inner, near, og, got, pixels[None]
    )
    grad_wout, grad_win, grad_taps, grad_gain, grad_shift = call(
        functools.partial(unpack_kernel, norm_scale),
        (
            shape((HID, C), F32),
            shape((C, HID), F32),
            shape(kernel.shape, F32),
            shape((1, C), F32),
            shape((1, C), F32),
        ),
    )(wide)
    return (
        result[None],
        grad_input[None],
        grad_taps,
        grad_gain[0],
        grad_shift[0],
        grad_win,
        grad_wout,
    )


def solution(mesh):
    return jax.shard_map(
        body,
        mesh=mesh,
        in_specs=(P("rep", "face"), P("rep", "face")) + (P(),) * 9,
        out_specs=(P("rep", "face"), P("rep", "face")) + (P(),) * 5,
        check_vma=False,
    )
```

```python
import functools
import math

import jax
import jax.numpy as jnp
import numpy as np
from jax import lax
from jax.experimental import pallas as pl
from jax.experimental.pallas import tpu as pltpu
from jax.sharding import PartitionSpec as P

BF = jnp.bfloat16
F32 = jnp.float32
N = 32
J = 16
C = 256
HALF = 128
HID = 1024
T = 2
PARTS = 16
KB = 48
SENT = PARTS * KB
LOCAL = 2 * 3 * N
SIDE = 8
MIB = 1024 * 1024


def band_pixel(e, r, p):
    return ((r, p), (p, N - 1 - r), (N - 1 - r, N - 1 - p), (N - 1 - p, r))[e]


def turned_pixel(e, i, j):
    last = N + 5
    return ((i, j), (j, last - i), (last - i, last - j), (last - j, i))[e]


def block_of(e):
    return (0, 1, 0, 2)[e]


def edge_of(t, block):
    return ((0, 1, 3), (2, 1, 3))[t][block]


def chunk_row(t, e, r, p):
    return (p // 2) * KB + block_of(e) * 16 + t * 6 + (p % 2) * 3 + r


def corner_row(t, e, r, c):
    return (r * 3 + c) * KB + t * 16 + 12 + e


def source_pixels():
    pixels = np.full((SENT,), -1, np.int32)
    for t in range(T):
        for e in range(4):
            for r in range(3):
                if e != 2 - 2 * t:
                    for p in range(N):
                        y, x = band_pixel(e, r, p)
                        pixels[chunk_row(t, e, r, p)] = t * N * N + y * N + x
                for c in range(3):
                    y, x = band_pixel(e, r, c)
                    pixels[corner_row(t, e, r, c)] = t * N * N + y * N + x
    return pixels


def rim_sources(t):
    table = {}
    for e in range(4):
        for i in range(3):
            for j in range(N):
                pixel = turned_pixel(e, i, j + 3)
                if e == 2 - 2 * t:
                    y, x = band_pixel((e + 2) % 4, 2 - i, j)
                    y = y if t == 0 else y - (N - 3)
                    row = SENT + t * 3 * N + y * N + x
                    table[pixel] = (e, row, row)
                else:
                    flipped = chunk_row(t, e, 2 - i, N - 1 - j)
                    table[pixel] = (e, chunk_row(t, e, 2 - i, j), flipped)
            for j in range(3):
                pixel = turned_pixel(e, i, j)
                table[pixel] = (
                    4 + e,
                    corner_row(t, e, 2 - i, 2 - j),
                    corner_row(t, e, 2 - j, 2 - i),
                )
    return table


def tables_of(pixels):
    tables = [rim_sources(t) for t in range(T)]
    piece = np.zeros((len(pixels), T * 8), np.int32)
    plain = np.full((len(pixels),), -1, np.int32)
    flipped = np.full((len(pixels),), -1, np.int32)
    for row, (t, p, q) in enumerate(pixels):
        if (p, q) in tables[t]:
            which, plain[row], flipped[row] = tables[t][p, q]
            piece[row, t * 8 + which] = 1
    return piece, plain, flipped


def rows_of(tables, flags):
    piece, plain, flipped = tables
    is_flipped = jnp.sum(piece * flags.reshape(1, -1), axis=1) > 0
    return jnp.where(is_flipped, flipped, plain)


def forward_rim_pixels():
    rows = [(t, p, q + 3) for p in (0, 1, 2, 35, 36, 37) for t in range(T) for q in range(N)]
    for p in range(N + 6):
        for t in range(T):
            rows += [(t, p, q) for q in (0, 1, 2, 35, 36, 37)] + [(t, -9, -9)] * 2
    return rows


RIM_PAIRS = (-2, -1, 16, 17)


def backward_rim_pixels():
    rows = []
    for u in range(2):
        for p in (0, 1, 2, 35, 36, 37):
            rows += [(t, p, 3 + 2 * j + u) for t in range(T) for j in range(J)]
        for k in range(19):
            for v in range(2):
                rows += [(t, 2 * k + v, 3 + 2 * j + u) for t in range(T) for j in RIM_PAIRS]
        rows += [(0, -9, -9)] * 16
    return rows


def pair_selector():
    sel = np.zeros((4, 128, 4 * (N + SIDE)), np.float32)
    for d in range(4):
        for s in range(2):
            for j in range(J):
                q = 2 * (j + d) + s
                for at in range(4):
                    if q < 3:
                        column = 4 * N + at * SIDE + q
                    elif q < N + 3:
                        column = at * N + q - 3
                    else:
                        column = 4 * N + at * SIDE + q - N
                    sel[at, d * 32 + s * 16 + j, column] = 1
    return sel.reshape(512, 4 * (N + SIDE))


def grad_selector():
    sel = np.zeros((768, 3, T, 32), np.float32)
    for d in range(4):
        for s in range(2):
            for j in range(J):
                col = 2 * (j + d) + s - 3
                if 0 <= col < N:
                    for v in range(2):
                        for t in range(T):
                            row = (v * T + t) * 128 + d * 32 + s * 16 + j
                            sel[row, 1 + v, t, (col % 2) * 16 + col // 2] = 1
    rim = grad_rim_selector().reshape(128, 2, T, 32)
    sel[512:640, 1:3] = rim
    sel[640:768, 0:2] = rim
    return sel.reshape(768, 192)


def grad_rim_selector():
    sel = np.zeros((128, 128), np.float32)
    for d in range(4):
        for s in range(2):
            for v in range(2):
                for t in range(T):
                    for at, j in enumerate(RIM_PAIRS):
                        col = 2 * (j + d) + s - 3
                        if 0 <= col < N:
                            row = (d * 2 + s) * 16 + v * 8 + t * 4 + at
                            sel[row, v * 64 + t * 32 + (col % 2) * 16 + col // 2] = 1
    return sel


def split_columns():
    sel = np.zeros((256, 256), np.float32)
    for r in range(8):
        for col in range(N):
            sel[r * 32 + (col % 2) * 16 + col // 2, r * 32 + col] = 1
    return sel


def dot(a, b):
    return jnp.dot(a, b, preferred_element_type=F32)


def fetch(pairs, sems):
    copies = [
        pltpu.make_async_copy(src, dst, sems.at[i]) for i, (src, dst) in enumerate(pairs)
    ]
    for copy in copies:
        copy.start()
    return copies


def column_of(row):
    return jnp.broadcast_to(row, (8, row.shape[1])).T[:, 0:1]


def pack_kernel(fields_in, pixel_in, out_ref, fields_ref, pixel_ref, sems):
    for copy in fetch([(pixel_in, pixel_ref), (fields_in, fields_ref)], sems):
        copy.wait()
    x = fields_ref[...].reshape(T * N * N, C)
    for m in range(4):
        rows = SENT // 4
        pixel = pixel_ref[m * rows : (m + 1) * rows]
        columns = lax.broadcasted_iota(jnp.int32, (rows, T * N * N), 1)
        pick = jnp.where(columns == pixel, 1.0, 0.0).astype(BF)
        out_ref[m * 4 : (m + 1) * 4] = dot(pick, x).astype(BF).reshape(4, KB, C)


def order_kernel(fields_ref, og_ref, split_ref, x_ref, o_ref):
    for m in range(4):
        for t in range(T):
            rows = slice(m * 8, (m + 1) * 8)
            for src, dst in ((fields_ref, x_ref), (og_ref, o_ref)):
                block = src[t, rows].reshape(256, C)
                dst[rows, t * 32 : (t + 1) * 32] = (
                    dot(split_ref[...], block).astype(BF).reshape(8, 32, C)
                )


def build_weights(kern_ref, w_ref, mirrored, halves=(0, 1)):
    eye = lax.broadcasted_iota(jnp.int32, (HALF, HALF), 0) == lax.broadcasted_iota(
        jnp.int32, (HALF, HALF), 1
    )
    zero = jnp.zeros((HALF, HALF), BF)

    def step(a, carry):
        row = 6 - a if mirrored else a
        taps = kern_ref[row]
        for at, h in enumerate(halves):
            blocks = [
                jnp.where(eye, taps[b : b + 1, h * HALF : (h + 1) * HALF], 0.0).astype(BF)
                for b in range(7)
            ]
            if mirrored:
                blocks = blocks[::-1]
            for d in range(4):
                for s in range(2):
                    for u in range(2):
                        b = 2 * d + s - u
                        block = blocks[b] if 0 <= b <= 6 else zero
                        top = d * 256 + s * HALF
                        w_ref[at, a, top : top + HALF, u * HALF : (u + 1) * HALF] = block
        return carry

    lax.fori_loop(0, 7, step, 0)


def spread(picked, q_ref, index, base):
    rows = picked.shape[0] // 8
    for d in range(4):
        for s in range(2):
            at = (d * 2 + s) * rows
            for h in range(2):
                lane = d * 256 + s * HALF
                q_ref[h, index, base : base + rows, lane : lane + HALF] = picked[
                    at : at + rows, h * HALF : (h + 1) * HALF
                ]


def forward_kernel(
    fields_in,
    x_in,
    o_in,
    recv_in,
    row_ref,
    kern_ref,
    gain_ref,
    shift_ref,
    win_in,
    wout_in,
    win_t_in,
    wout_t_in,
    psel_in,
    merge_in,
    result_out,
    wide_out,
    gz_out,
    fields_ref,
    recv_ref,
    win_ref,
    wout_ref,
    win_t_ref,
    wout_t_ref,
    psel_ref,
    merge_ref,
    result_ref,
    gz_ref,
    wide_ref,
    mid_ref,
    side_ref,
    q_ref,
    w_ref,
    x_ref,
    o_ref,
    z_ref,
    gwin_ref,
    gwout_ref,
    gains_ref,
    g_ref,
    gt_ref,
    small_ref,
    sems,
):
    copies = fetch(
        [
            (recv_in, recv_ref),
            (fields_in, fields_ref),
            (psel_in, psel_ref),
        ],
        sems,
    )
    build_weights(kern_ref, w_ref, False)
    for copy in copies:
        copy.wait()
    copies = fetch(
        [
            (x_in, x_ref),
            (o_in, o_ref),
            (win_in, win_ref),
            (wout_in, wout_ref),
            (win_t_in, win_t_ref),
            (wout_t_in, wout_t_ref),
            (merge_in, merge_ref),
        ],
        sems,
    )
    source = jnp.concatenate(
        [
            recv_ref[...].reshape(SENT, C),
            fields_ref[1, 0:3].reshape(3 * N, C),
            fields_ref[0, N - 3 :].reshape(3 * N, C),
        ],
        axis=0,
    )
    outer = 6 * T * N
    row = column_of(row_ref[...])
    columns = lax.broadcasted_iota(jnp.int32, (row.shape[0], SENT + LOCAL), 1)
    pick = jnp.where(columns == row, 1.0, 0.0).astype(BF)
    rims = dot(pick, source)
    rims, sides = rims[:outer].astype(BF).reshape(6, T, N, C), rims[outer:]
    mid_ref[0:3] = rims[0:3]
    mid_ref[N + 3 :] = rims[3:6]
    side_ref[...] = sides.astype(BF).reshape(N + 6, T * SIDE, C)
    for t in range(T):
        mid_ref[3 : N + 3, t] = fields_ref[t]

    def pairs(i, carry):
        block = jnp.concatenate(
            [
                mid_ref[pl.ds(2 * i, 2)].reshape(4 * N, C),
                side_ref[pl.ds(2 * i, 2)].reshape(4 * SIDE, C),
            ],
            axis=0,
        )
        picked = dot(psel_ref[...], block).astype(BF)
        for v in range(2):
            for t in range(T):
                at = (v * T + t) * 128
                spread(picked[at : at + 128], q_ref, 2 * i + v, t * 16)
        return carry

    for i in range((N + 6) // 2):
        pairs(i, 0)

    def conv(m, carry):
        for h in range(2):
            acc = None
            for a in range(7):
                lhs = q_ref[h, pl.ds(m * 8 + a, 8)].reshape(256, 1024)
                part = dot(lhs, w_ref[h, a])
                acc = part if acc is None else acc + part
            acc = acc.reshape(8, T, 16, 256)
            for t in range(T):
                for u in range(2):
                    base = t * 32 + u * 16
                    z_ref[
                        pl.ds(m * 8, 8), base : base + 16, h * HALF : (h + 1) * HALF
                    ] = acc[:, t, :, u * HALF : (u + 1) * HALF]
        return carry

    lax.fori_loop(0, 4, conv, 0)

    for copy in copies:
        copy.wait()
    gwin_ref[...] = jnp.zeros_like(gwin_ref)
    gwout_ref[...] = jnp.zeros_like(gwout_ref)
    gains_ref[...] = jnp.zeros_like(gains_ref)
    gz_ref[0] = jnp.zeros((64, C), BF)
    gz_ref[N + 1] = jnp.zeros((64, C), BF)
    gain = gain_ref[...]
    shift = shift_ref[...]

    def mlp(m, carry):
        rows = pl.ds(m * 8, 8)
        z = z_ref[rows].reshape(512, C)
        average = jnp.mean(z, axis=1, keepdims=True)
        centered = z - average
        variance = jnp.mean(centered * centered, axis=1, keepdims=True)
        inv_std = lax.rsqrt(variance + 1e-06)
        normed = centered * inv_std
        zn = (normed * gain + shift).astype(BF)
        og = o_ref[rows].reshape(512, C)
        hidden = dot(zn, win_ref[...])
        cdf = 0.5 * (1.0 + lax.erf(hidden * (1.0 / math.sqrt(2.0))))
        pdf = jnp.exp(-0.5 * hidden * hidden) * (1.0 / math.sqrt(2.0 * math.pi))
        act = (hidden * cdf).astype(BF)
        slope = cdf + hidden * pdf
        out = x_ref[rows].reshape(512, C).astype(F32) + dot(act, wout_ref[...])
        x_ref[rows] = out.astype(BF).reshape(8, 64, C)
        grad_hidden = (dot(og, wout_t_ref[...]) * slope).astype(BF)
        gwout_ref[...] += dot(og.T, act)
        gwin_ref[...] += dot(zn.T, grad_hidden)
        grad_normed = dot(grad_hidden, win_t_ref[...])
        gains_ref[0:8] += jnp.sum((grad_normed * normed).reshape(64, 8, C), axis=0)
        gains_ref[8:16] += jnp.sum(grad_normed.reshape(64, 8, C), axis=0)
        scaled = grad_normed * gain
        grad_z = inv_std * (
            scaled
            - jnp.mean(scaled, axis=1, keepdims=True)
            - normed * jnp.mean(scaled * normed, axis=1, keepdims=True)
        )
        grad_z = grad_z.astype(BF).reshape(8, 64, C)
        gz_ref[pl.ds(m * 8 + 1, 8)] = grad_z
        for h in range(2):
            for t in range(T):
                for u in range(2):
                    g_ref[h, rows, t * 16 : (t + 1) * 16, u * HALF : (u + 1) * HALF] = grad_z[
                        :, t * 32 + u * 16 : t * 32 + u * 16 + 16, h * HALF : (h + 1) * HALF
                    ]
        return carry

    for m in range(4):
        mlp(m, 0)

    def unorder(m, carry):
        for t in range(T):
            rows = pl.ds(m * 8, 8)
            block = x_ref[rows, t * 32 : (t + 1) * 32].reshape(256, C)
            result_ref[t, rows] = dot(merge_ref[...], block).astype(BF).reshape(8, 32, C)
        return carry

    for m in range(4):
        unorder(m, 0)
    half = wide_ref.shape[0] // 2
    wide_ref[:half, 0:256] = gwout_ref[...].T.astype(BF).reshape(half, 256, C)
    wide_ref[half:, 0:256] = gwin_ref[...].T.astype(BF).reshape(half, 256, C)
    copies = fetch(
        [
            (wide_ref.at[:, 0:256], wide_out.at[:, 0:256]),
            (result_ref, result_out),
            (gz_ref, gz_out),
        ],
        sems,
    )

    for h in range(2):
        gt_ref[h] = g_ref[h].reshape(1024, 256).T
    eye = lax.broadcasted_iota(jnp.int32, (HALF, HALF), 0) == lax.broadcasted_iota(
        jnp.int32, (HALF, HALF), 1
    )

    def taps(a, carry):
        for h in range(2):
            prod = dot(gt_ref[h], q_ref[h, pl.ds(a, 32)].reshape(1024, 1024))
            sums = [None] * 7
            for d in range(4):
                for s in range(2):
                    for u in range(2):
                        b = 2 * d + s - u
                        if 0 <= b <= 6:
                            lane = d * 256 + s * HALF
                            block = jnp.where(
                                eye, prod[u * HALF : (u + 1) * HALF, lane : lane + HALF], 0.0
                            )
                            sums[b] = block if sums[b] is None else sums[b] + block
            rows = [jnp.sum(block, axis=0, keepdims=True) for block in sums]
            rows.append(jnp.zeros((1, HALF), F32))
            small_ref[a, :, h * HALF : (h + 1) * HALF] = jnp.concatenate(rows, axis=0)
        return carry

    for a in range(7):
        taps(a, 0)
    small_ref[7] = jnp.concatenate(
        [
            jnp.sum(gains_ref[0:8], axis=0, keepdims=True),
            jnp.sum(gains_ref[8:16], axis=0, keepdims=True),
            jnp.zeros((6, C), F32),
        ],
        axis=0,
    )
    blank = jnp.zeros((8, 8, C), F32)
    wide_ref[:, 256:272] = jnp.concatenate([small_ref[...], blank], axis=1).astype(BF)
    copies += fetch([(wide_ref.at[:, 256:272], wide_out.at[:, 256:272])], sems.at[3:4])
    for copy in copies:
        copy.wait()


def rims_kernel(
    gz_ref,
    kern_ref,
    row_ref,
    gsel_ref,
    rsel_ref,
    sent_ref,
    near_ref,
    w_ref,
    g_ref,
    r_ref,
    edge_ref,
):
    build_weights(kern_ref, w_ref, True)
    for h in range(2):
        g_ref[h, 0:6] = jnp.zeros((6, 32, 1024), BF)
        g_ref[h, 12:18] = jnp.zeros((6, 32, 1024), BF)
        r_ref[0, h, 0:3] = jnp.zeros((3, 16, 1024), BF)
        r_ref[0, h, 19:22] = jnp.zeros((3, 16, 1024), BF)
        r_ref[1, h, 0:2] = jnp.zeros((2, 16, 1024), BF)
        r_ref[1, h, 19:22] = jnp.zeros((3, 16, 1024), BF)

    def rim_pairs(i, carry):
        block = gz_ref[pl.ds(2 * i, 3)].reshape(192, C)
        picked = dot(gsel_ref[512:], block).astype(BF)
        spread(picked[0:128], r_ref.at[0], 3 + i, 0)
        spread(picked[128:256], r_ref.at[1], 2 + i, 0)
        return carry

    for i in range(16):
        rim_pairs(i, 0)
    last = dot(rsel_ref[...], gz_ref[N : N + 2].reshape(128, C)).astype(BF)
    spread(last, r_ref.at[1], 18, 0)
    for first, row in ((0, 6), (1, 7), (29, 9), (30, 10)):
        picked = dot(gsel_ref[0:512], gz_ref[first : first + 3].reshape(192, C)).astype(BF)
        for v in range(2):
            for t in range(T):
                at = (v * T + t) * 128
                spread(picked[at : at + 128], g_ref, row + v, t * 16)

    for h in range(2):
        acc = None
        for a in range(7):
            k, v = a // 2, a % 2
            lhs = jnp.concatenate(
                [
                    g_ref[h, a : a + 3].reshape(96, 1024),
                    g_ref[h, 9 + a : 12 + a].reshape(96, 1024),
                    r_ref[v, h, k : k + 19].reshape(304, 1024),
                ],
                axis=0,
            )
            part = dot(lhs, w_ref[h, a])
            acc = part if acc is None else acc + part
        edge_ref[h, 0:496] = acc.astype(BF)
        edge_ref[h, 496:512] = jnp.zeros((16, 256), BF)

    edges = jnp.concatenate(
        [
            jnp.concatenate([edge_ref[0, :, 0:HALF], edge_ref[1, :, 0:HALF]], axis=1),
            jnp.concatenate([edge_ref[0, :, HALF:], edge_ref[1, :, HALF:]], axis=1),
        ],
        axis=0,
    )
    rows = SENT + LOCAL
    pick = lax.broadcasted_iota(jnp.int32, (rows, 1024), 0) == row_ref[...]
    back = dot(jnp.where(pick, 1.0, 0.0).astype(BF), edges)
    sent_ref[...] = back[:SENT].astype(BF).reshape(PARTS, KB, C)
    near_ref[...] = back[SENT:].reshape(2, 3, N, C)


def inside_kernel(h, gz_in, kern_ref, gsel_ref, inner_ref, w_ref, g_ref, gz_ref, sems):
    copies = fetch([(gz_in, gz_ref)], sems)
    build_weights(kern_ref, w_ref, True, (h,))
    g_ref[0:3] = jnp.zeros((3, 32, 1024), BF)
    g_ref[35:38] = jnp.zeros((3, 32, 1024), BF)
    copies[0].wait()

    def pairs(i, carry):
        block = gz_ref[pl.ds(2 * i, 3), :, h * HALF : (h + 1) * HALF].reshape(192, HALF)
        picked = dot(gsel_ref[0:512], block).astype(BF)
        for v in range(2):
            for t in range(T):
                for ds in range(8):
                    at = (v * T + t) * 128 + ds * 16
                    rows = slice(t * 16, (t + 1) * 16)
                    lanes = slice(ds * HALF, (ds + 1) * HALF)
                    g_ref[3 + 2 * i + v, rows, lanes] = picked[at : at + 16]
        return carry

    for i in range(16):
        pairs(i, 0)

    def inside(m, carry):
        acc = None
        for a in range(7):
            lhs = g_ref[pl.ds(m * 8 + a, 8)].reshape(256, 1024)
            part = dot(lhs, w_ref[0, a])
            acc = part if acc is None else acc + part
        acc = acc.reshape(8, T, 16, 256)
        for t in range(T):
            for u in range(2):
                inner_ref[t, pl.ds(m * 8, 8), pl.ds(u, 16, stride=2), :] = acc[
                    :, t, :, u * HALF : (u + 1) * HALF
                ]
        return carry

    lax.fori_loop(0, 4, inside, 0)


def join_kernel(sent_ref, wide_ref, out_ref):
    total = wide_ref[0].astype(F32)
    for rep in range(1, wide_ref.shape[0]):
        total = total + wide_ref[rep].astype(F32)
    total = total.astype(BF)
    out_ref[:, 0:KB] = sent_ref[...]
    out_ref[:, KB : KB + 16] = total[0:256].reshape(PARTS, 16, C)
    for part in range(PARTS):
        out_ref[part, KB + 16 :] = total[256:272]


def return_kernel(got_ref, source_ref, out_ref, small_ref):
    pick = lax.broadcasted_iota(jnp.int32, (SENT, SENT), 0) == source_ref[...]
    pick = jnp.where(pick, 1.0, 0.0).astype(BF)
    routed = dot(pick, got_ref[:, 0:KB].reshape(SENT, C)).astype(BF)
    out_ref[:, 0:KB] = routed.reshape(PARTS, KB, C)
    total = got_ref[0, KB:].astype(F32)
    for part in range(1, PARTS):
        total = total + got_ref[part, KB:].astype(F32)
    total = total.astype(BF)
    small_ref[...] = total[16:]
    for part in range(PARTS):
        out_ref[part, KB:] = total[:16]


def spread_kernel(got_ref, small_ref, out_ref):
    wide = got_ref[:, KB : KB + 16].reshape(256, C)
    small = small_ref[...]
    for rep in range(out_ref.shape[0]):
        out_ref[rep, 0:256] = wide
        out_ref[rep, 256:272] = small


def final_kernel(inner0_ref, inner1_ref, near_ref, og_ref, recv_ref, pixel_ref, out_ref):
    recv = recv_ref[:, 0:KB].reshape(SENT, C)
    for t in range(T):
        for m in range(2):
            rows = N * N // 2
            first = (t * 2 + m) * rows
            pick = lax.broadcasted_iota(jnp.int32, (rows, SENT), 0) + first == pixel_ref[...]
            back = dot(jnp.where(pick, 1.0, 0.0).astype(BF), recv).reshape(N // 2, N, C)
            half = slice(m * N // 2, (m + 1) * N // 2)
            inner = jnp.concatenate([inner0_ref[t, half], inner1_ref[t, half]], axis=2)
            total = inner + og_ref[t, half].astype(F32) + back
            if (t, m) == (1, 0):
                total = jnp.concatenate([total[:3] + near_ref[0], total[3:]], axis=0)
            if (t, m) == (0, 1):
                total = jnp.concatenate([total[:-3], total[-3:] + near_ref[1]], axis=0)
            out_ref[t, half] = total.astype(BF)


def unpack_kernel(norm_scale, got_ref, wout_ref, win_ref, taps_ref, gain_ref, shift_ref):
    half = got_ref.shape[0] // 2
    small = got_ref[:, 256:272].astype(F32) * norm_scale
    taps_ref[...] = small[0:7, 0:7]
    gain_ref[...] = small[7, 0:1]
    shift_ref[...] = small[7, 1:2]
    for rep in range(half):
        rows = slice(rep * 256, (rep + 1) * 256)
        wout_ref[rows] = got_ref[rep, 0:256].astype(F32) * norm_scale
        win_ref[:, rows] = (got_ref[half + rep, 0:256].astype(F32) * norm_scale).T


def call(kernel, outs, scratch=(), out_specs=None, in_specs=None, flops=0, vmem=16):
    options = {}
    if flops:
        options["cost_estimate"] = pl.CostEstimate(
            flops=flops, bytes_accessed=10_000_000, transcendentals=0
        )
    if in_specs is not None:
        options["in_specs"] = in_specs
    if out_specs is not None:
        options["out_specs"] = out_specs
    return pl.pallas_call(
        kernel,
        out_shape=outs,
        scratch_shapes=list(scratch),
        compiler_params=pltpu.CompilerParams(vmem_limit_bytes=vmem * MIB),
        **options,
    )


def swap(array, axes):
    return lax.all_to_all(array, axes, 0, 0, tiled=True)


def body(
    fields,
    out_grad,
    kernel,
    ln_gain,
    ln_shift,
    w_in,
    w_out,
    edge_tile,
    edge_code,
    corner_tile,
    corner_code,
):
    x = fields[0]
    og = out_grad[0]
    faces = lax.axis_size("face")
    reps = lax.axis_size("rep")
    devices = faces * reps
    norm_scale = 1.0 / math.sqrt(devices * T * N * N)
    offset = lax.axis_index("face") * T
    vm = pl.BlockSpec(memory_space=pltpu.VMEM)
    hbm = pl.BlockSpec(memory_space=pltpu.HBM)
    shape = jax.ShapeDtypeStruct

    codes = jnp.concatenate([edge_code, corner_code], axis=1) // 4
    flags = lax.dynamic_slice_in_dim(codes, offset, T, 0)
    odd = jnp.arange(edge_tile.shape[0]) % T
    blocks = []
    for block in range(3):
        edge = [edge_of(t, block) for t in range(T)]
        tile = jnp.where(odd == 0, edge_tile[:, edge[0]], edge_tile[:, edge[1]])
        code = jnp.where(odd == 0, edge_code[:, edge[0]], edge_code[:, edge[1]]) % 4
        place = jnp.where(code == 1, 16, jnp.where(code == 3, 32, 0))
        first = tile // T * KB + place + tile % T * 6
        blocks.append((first[:, None] + np.arange(6)).reshape(-1, 12))
    corners = corner_tile // T * KB + corner_tile % T * 16 + 12 + corner_code % 4
    corners = corners.reshape(-1, T, 4)
    none = jnp.full_like(corners[:, 0], -1)
    source = jnp.concatenate(
        [blocks[0], corners[:, 0], blocks[1], corners[:, 1], blocks[2], none], axis=1
    ).reshape(-1)
    pick = (source[:, None] == jnp.arange(SENT, dtype=jnp.int32)).astype(BF)
    rim_rows = rows_of(tables_of(forward_rim_pixels()), flags)
    edge_rows = rows_of(tables_of(backward_rim_pixels()), flags)
    pixels = source_pixels()

    taps = jnp.pad(kernel.astype(F32), ((0, 0), (0, 1), (0, 0)))

    sent = call(
        pack_kernel,
        shape((PARTS, KB, C), BF),
        scratch=(
            pltpu.VMEM((T, N, N, C), BF),
            pltpu.VMEM((SENT, 1), jnp.int32),
            pltpu.SemaphoreType.DMA((2,)),
        ),
        in_specs=[hbm, hbm],
        out_specs=vm,
        vmem=60,
    )(x, pixels[:, None])
    split = split_columns()
    ordered = shape((N, 64, C), BF)
    x_ord, og_ord = call(order_kernel, (ordered, ordered), flops=3_000_000_000)(
        x, og, split.astype(BF)
    )
    got = swap(sent, "face")
    routed = dot(pick, got.reshape(-1, C)).astype(BF).reshape(got.shape)
    got = swap(routed, "face")

    result, wide, gz = call(
        forward_kernel,
        (
            shape((T, N, N, C), BF),
            shape((reps, 272, C), BF),
            shape((N + 2, 64, C), BF),
        ),
        scratch=(
            pltpu.VMEM((T, N, N, C), BF),
            pltpu.VMEM((PARTS, KB, C), BF),
            pltpu.VMEM((C, HID), BF),
            pltpu.VMEM((HID, C), BF),
            pltpu.VMEM((HID, C), BF),
            pltpu.VMEM((C, HID), BF),
            pltpu.VMEM((512, 4 * (N + SIDE)), BF),
            pltpu.VMEM((256, 256), BF),
            pltpu.VMEM((T, N, N, C), BF),
            pltpu.VMEM((N + 2, 64, C), BF),
            pltpu.VMEM((reps, 272, C), BF),
            pltpu.VMEM((N + 6, T, N, C), BF),
            pltpu.VMEM((N + 6, T * SIDE, C), BF),
            pltpu.VMEM((2, N + 6, 32, 1024), BF),
            pltpu.VMEM((2, 7, 1024, 256), BF),
            pltpu.VMEM((N, 64, C), BF),
            pltpu.VMEM((N, 64, C), BF),
            pltpu.VMEM((N, 64, C), F32),
            pltpu.VMEM((C, HID), F32),
            pltpu.VMEM((C, HID), F32),
            pltpu.VMEM((16, C), F32),
            pltpu.VMEM((2, N, 32, 256), BF),
            pltpu.VMEM((2, 256, 1024), BF),
            pltpu.VMEM((8, 8, C), F32),
            pltpu.SemaphoreType.DMA((7,)),
        ),
        in_specs=[hbm] * 4 + [vm] * 4 + [hbm] * 6,
        out_specs=(hbm, hbm, hbm),
        flops=40_000_000_000,
        vmem=60,
    )(
        x,
        x_ord,
        og_ord,
        got,
        rim_rows[None],
        taps,
        ln_gain[None],
        ln_shift[None],
        w_in,
        w_out,
        w_in.T,
        w_out.T,
        pair_selector().astype(BF),
        split.T.astype(BF),
    )

    wide = swap(wide, "rep")
    gsel = grad_selector().astype(BF)
    sent, near = call(
        rims_kernel,
        (shape((PARTS, KB, C), BF), shape((2, 3, N, C), F32)),
        scratch=(
            pltpu.VMEM((2, 7, 1024, 256), BF),
            pltpu.VMEM((2, 18, 32, 1024), BF),
            pltpu.VMEM((2, 2, 22, 16, 1024), BF),
            pltpu.VMEM((2, 512, 256), BF),
        ),
        flops=12_000_000_000,
        vmem=32,
    )(gz, taps, edge_rows[None], gsel, grad_rim_selector().astype(BF))
    inner = [
        call(
            functools.partial(inside_kernel, h),
            shape((T, N, N, HALF), F32),
            scratch=(
                pltpu.VMEM((1, 7, 1024, 256), BF),
                pltpu.VMEM((N + 6, 32, 1024), BF),
                pltpu.VMEM((N + 2, 64, C), BF),
                pltpu.SemaphoreType.DMA((1,)),
            ),
            in_specs=[hbm, vm, vm],
            out_specs=vm,
            flops=9_000_000_000,
            vmem=20,
        )(gz, taps, gsel)
        for h in range(2)
    ]
    sent = call(join_kernel, shape((PARTS, KB + 32, C), BF))(sent, wide)
    got = swap(sent, "face")
    routed, small = call(
        return_kernel, (shape((PARTS, KB + 16, C), BF), shape((16, C), BF))
    )(got, source[None])
    got = swap(routed, "face")
    wide = call(spread_kernel, shape((reps, 272, C), BF))(got, small)
    wide = swap(wide, "rep")
    grad_input = call(final_kernel, shape((T, N, N, C), BF), flops=5_000_000_000)(
        *inner, near, og, got, pixels[None]
    )
    grad_wout, grad_win, grad_taps, grad_gain, grad_shift = call(
        functools.partial(unpack_kernel, norm_scale),
        (
            shape((HID, C), F32),
            shape((C, HID), F32),
            shape(kernel.shape, F32),
            shape((1, C), F32),
            shape((1, C), F32),
        ),
    )(wide)
    return (
        result[None],
        grad_input[None],
        grad_taps,
        grad_gain[0],
        grad_shift[0],
        grad_win,
        grad_wout,
    )


def solution(mesh):
    return jax.shard_map(
        body,
        mesh=mesh,
        in_specs=(P("rep", "face"), P("rep", "face")) + (P(),) * 9,
        out_specs=(P("rep", "face"), P("rep", "face")) + (P(),) * 5,
        check_vma=False,
    )
```

```python
import functools
import math

import jax
import jax.numpy as jnp
import numpy as np
from jax import lax
from jax.experimental import pallas as pl
from jax.experimental.pallas import tpu as pltpu
from jax.sharding import PartitionSpec as P

BF = jnp.bfloat16
F32 = jnp.float32
N = 32
J = 16
C = 256
HALF = 128
HID = 1024
T = 2
PARTS = 16
KB = 48
SENT = PARTS * KB
LOCAL = 2 * 3 * N
SIDE = 8
MIB = 1024 * 1024


def band_pixel(e, r, p):
    return ((r, p), (p, N - 1 - r), (N - 1 - r, N - 1 - p), (N - 1 - p, r))[e]


def turned_pixel(e, i, j):
    last = N + 5
    return ((i, j), (j, last - i), (last - i, last - j), (last - j, i))[e]


def block_of(e):
    return (0, 1, 0, 2)[e]


def edge_of(t, block):
    return ((0, 1, 3), (2, 1, 3))[t][block]


def chunk_row(t, e, r, p):
    return (p // 2) * KB + block_of(e) * 16 + t * 6 + (p % 2) * 3 + r


def corner_row(t, e, r, c):
    return (r * 3 + c) * KB + t * 16 + 12 + e


def source_pixels():
    pixels = np.full((SENT,), -1, np.int32)
    for t in range(T):
        for e in range(4):
            for r in range(3):
                if e != 2 - 2 * t:
                    for p in range(N):
                        y, x = band_pixel(e, r, p)
                        pixels[chunk_row(t, e, r, p)] = t * N * N + y * N + x
                for c in range(3):
                    y, x = band_pixel(e, r, c)
                    pixels[corner_row(t, e, r, c)] = t * N * N + y * N + x
    return pixels


def rim_sources(t):
    table = {}
    for e in range(4):
        for i in range(3):
            for j in range(N):
                pixel = turned_pixel(e, i, j + 3)
                if e == 2 - 2 * t:
                    y, x = band_pixel((e + 2) % 4, 2 - i, j)
                    y = y if t == 0 else y - (N - 3)
                    row = SENT + t * 3 * N + y * N + x
                    table[pixel] = (e, row, row)
                else:
                    flipped = chunk_row(t, e, 2 - i, N - 1 - j)
                    table[pixel] = (e, chunk_row(t, e, 2 - i, j), flipped)
            for j in range(3):
                pixel = turned_pixel(e, i, j)
                table[pixel] = (
                    4 + e,
                    corner_row(t, e, 2 - i, 2 - j),
                    corner_row(t, e, 2 - j, 2 - i),
                )
    return table


def tables_of(pixels):
    tables = [rim_sources(t) for t in range(T)]
    piece = np.zeros((len(pixels), T * 8), np.int32)
    plain = np.full((len(pixels),), -1, np.int32)
    flipped = np.full((len(pixels),), -1, np.int32)
    for row, (t, p, q) in enumerate(pixels):
        if (p, q) in tables[t]:
            which, plain[row], flipped[row] = tables[t][p, q]
            piece[row, t * 8 + which] = 1
    return piece, plain, flipped


def rows_of(tables, flags):
    piece, plain, flipped = tables
    is_flipped = jnp.sum(piece * flags.reshape(1, -1), axis=1) > 0
    return jnp.where(is_flipped, flipped, plain)


def forward_rim_pixels():
    rows = [(t, p, q + 3) for p in (0, 1, 2, 35, 36, 37) for t in range(T) for q in range(N)]
    for p in range(N + 6):
        for t in range(T):
            rows += [(t, p, q) for q in (0, 1, 2, 35, 36, 37)] + [(t, -9, -9)] * 2
    return rows


RIM_PAIRS = (-2, -1, 16, 17)


def backward_rim_pixels():
    rows = []
    for u in range(2):
        for p in (0, 1, 2, 35, 36, 37):
            rows += [(t, p, 3 + 2 * j + u) for t in range(T) for j in range(J)]
        for k in range(19):
            for v in range(2):
                rows += [(t, 2 * k + v, 3 + 2 * j + u) for t in range(T) for j in RIM_PAIRS]
        rows += [(0, -9, -9)] * 16
    return rows


def pair_selector():
    sel = np.zeros((4, 128, 4 * (N + SIDE)), np.float32)
    for d in range(4):
        for s in range(2):
            for j in range(J):
                q = 2 * (j + d) + s
                for at in range(4):
                    if q < 3:
                        column = 4 * N + at * SIDE + q
                    elif q < N + 3:
                        column = at * N + q - 3
                    else:
                        column = 4 * N + at * SIDE + q - N
                    sel[at, d * 32 + s * 16 + j, column] = 1
    return sel.reshape(512, 4 * (N + SIDE))


def grad_selector():
    sel = np.zeros((768, 3, T, 32), np.float32)
    for d in range(4):
        for s in range(2):
            for j in range(J):
                col = 2 * (j + d) + s - 3
                if 0 <= col < N:
                    for v in range(2):
                        for t in range(T):
                            row = (v * T + t) * 128 + d * 32 + s * 16 + j
                            sel[row, 1 + v, t, (col % 2) * 16 + col // 2] = 1
    rim = grad_rim_selector().reshape(128, 2, T, 32)
    sel[512:640, 1:3] = rim
    sel[640:768, 0:2] = rim
    return sel.reshape(768, 192)


def grad_rim_selector():
    sel = np.zeros((128, 128), np.float32)
    for d in range(4):
        for s in range(2):
            for v in range(2):
                for t in range(T):
                    for at, j in enumerate(RIM_PAIRS):
                        col = 2 * (j + d) + s - 3
                        if 0 <= col < N:
                            row = (d * 2 + s) * 16 + v * 8 + t * 4 + at
                            sel[row, v * 64 + t * 32 + (col % 2) * 16 + col // 2] = 1
    return sel


def split_columns():
    sel = np.zeros((256, 256), np.float32)
    for r in range(8):
        for col in range(N):
            sel[r * 32 + (col % 2) * 16 + col // 2, r * 32 + col] = 1
    return sel


def dot(a, b):
    return jnp.dot(a, b, preferred_element_type=F32)


def fetch(pairs, sems):
    copies = [
        pltpu.make_async_copy(src, dst, sems.at[i]) for i, (src, dst) in enumerate(pairs)
    ]
    for copy in copies:
        copy.start()
    return copies


def column_of(row):
    return jnp.broadcast_to(row, (8, row.shape[1])).T[:, 0:1]


def pack_kernel(fields_in, pixel_in, out_ref, fields_ref, pixel_ref, sems):
    for copy in fetch([(pixel_in, pixel_ref), (fields_in, fields_ref)], sems):
        copy.wait()
    x = fields_ref[...].reshape(T * N * N, C)
    for m in range(4):
        rows = SENT // 4
        pixel = pixel_ref[m * rows : (m + 1) * rows]
        columns = lax.broadcasted_iota(jnp.int32, (rows, T * N * N), 1)
        pick = jnp.where(columns == pixel, 1.0, 0.0).astype(BF)
        out_ref[m * 4 : (m + 1) * 4] = dot(pick, x).astype(BF).reshape(4, KB, C)


def order_kernel(fields_ref, og_ref, split_ref, x_ref, o_ref):
    for m in range(4):
        for t in range(T):
            rows = slice(m * 8, (m + 1) * 8)
            for src, dst in ((fields_ref, x_ref), (og_ref, o_ref)):
                block = src[t, rows].reshape(256, C)
                dst[rows, t * 32 : (t + 1) * 32] = (
                    dot(split_ref[...], block).astype(BF).reshape(8, 32, C)
                )


def build_weights(kern_ref, w_ref, mirrored, halves=(0, 1)):
    eye = lax.broadcasted_iota(jnp.int32, (HALF, HALF), 0) == lax.broadcasted_iota(
        jnp.int32, (HALF, HALF), 1
    )
    zero = jnp.zeros((HALF, HALF), BF)

    def step(a, carry):
        row = 6 - a if mirrored else a
        taps = kern_ref[row]
        for at, h in enumerate(halves):
            blocks = [
                jnp.where(eye, taps[b : b + 1, h * HALF : (h + 1) * HALF], 0.0).astype(BF)
                for b in range(7)
            ]
            if mirrored:
                blocks = blocks[::-1]
            for d in range(4):
                for s in range(2):
                    for u in range(2):
                        b = 2 * d + s - u
                        block = blocks[b] if 0 <= b <= 6 else zero
                        top = d * 256 + s * HALF
                        w_ref[at, a, top : top + HALF, u * HALF : (u + 1) * HALF] = block
        return carry

    lax.fori_loop(0, 7, step, 0)


def spread(picked, q_ref, index, base):
    rows = picked.shape[0] // 8
    for d in range(4):
        for s in range(2):
            at = (d * 2 + s) * rows
            for h in range(2):
                lane = d * 256 + s * HALF
                q_ref[h, index, base : base + rows, lane : lane + HALF] = picked[
                    at : at + rows, h * HALF : (h + 1) * HALF
                ]


def forward_kernel(
    fields_in,
    x_in,
    o_in,
    recv_in,
    row_ref,
    kern_ref,
    gain_ref,
    shift_ref,
    win_in,
    wout_in,
    win_t_in,
    wout_t_in,
    psel_in,
    merge_in,
    result_out,
    wide_out,
    gz_out,
    fields_ref,
    recv_ref,
    win_ref,
    wout_ref,
    win_t_ref,
    wout_t_ref,
    psel_ref,
    merge_ref,
    result_ref,
    gz_ref,
    wide_ref,
    mid_ref,
    side_ref,
    q_ref,
    w_ref,
    x_ref,
    o_ref,
    z_ref,
    gwin_ref,
    gwout_ref,
    gains_ref,
    g_ref,
    gt_ref,
    small_ref,
    sems,
):
    copies = fetch(
        [
            (recv_in, recv_ref),
            (fields_in, fields_ref),
            (psel_in, psel_ref),
        ],
        sems,
    )
    build_weights(kern_ref, w_ref, False)
    for copy in copies:
        copy.wait()
    copies = fetch(
        [
            (x_in, x_ref),
            (o_in, o_ref),
            (win_in, win_ref),
            (wout_in, wout_ref),
            (win_t_in, win_t_ref),
            (wout_t_in, wout_t_ref),
            (merge_in, merge_ref),
        ],
        sems,
    )
    source = jnp.concatenate(
        [
            recv_ref[...].reshape(SENT, C),
            fields_ref[1, 0:3].reshape(3 * N, C),
            fields_ref[0, N - 3 :].reshape(3 * N, C),
        ],
        axis=0,
    )
    outer = 6 * T * N
    row = column_of(row_ref[...])
    columns = lax.broadcasted_iota(jnp.int32, (row.shape[0], SENT + LOCAL), 1)
    pick = jnp.where(columns == row, 1.0, 0.0).astype(BF)
    rims = dot(pick, source)
    rims, sides = rims[:outer].astype(BF).reshape(6, T, N, C), rims[outer:]
    mid_ref[0:3] = rims[0:3]
    mid_ref[N + 3 :] = rims[3:6]
    side_ref[...] = sides.astype(BF).reshape(N + 6, T * SIDE, C)
    for t in range(T):
        mid_ref[3 : N + 3, t] = fields_ref[t]

    def pairs(i, carry):
        block = jnp.concatenate(
            [
                mid_ref[pl.ds(2 * i, 2)].reshape(4 * N, C),
                side_ref[pl.ds(2 * i, 2)].reshape(4 * SIDE, C),
            ],
            axis=0,
        )
        picked = dot(psel_ref[...], block).astype(BF)
        for v in range(2):
            for t in range(T):
                at = (v * T + t) * 128
                spread(picked[at : at + 128], q_ref, 2 * i + v, t * 16)
        return carry

    for i in range((N + 6) // 2):
        pairs(i, 0)

    def conv(m, carry):
        for h in range(2):
            acc = None
            for a in range(7):
                lhs = q_ref[h, pl.ds(m * 8 + a, 8)].reshape(256, 1024)
                part = dot(lhs, w_ref[h, a])
                acc = part if acc is None else acc + part
            acc = acc.reshape(8, T, 16, 256)
            for t in range(T):
                for u in range(2):
                    base = t * 32 + u * 16
                    z_ref[
                        pl.ds(m * 8, 8), base : base + 16, h * HALF : (h + 1) * HALF
                    ] = acc[:, t, :, u * HALF : (u + 1) * HALF]
        return carry

    lax.fori_loop(0, 4, conv, 0)

    for copy in copies:
        copy.wait()
    gwin_ref[...] = jnp.zeros_like(gwin_ref)
    gwout_ref[...] = jnp.zeros_like(gwout_ref)
    gains_ref[...] = jnp.zeros_like(gains_ref)
    gz_ref[0] = jnp.zeros((64, C), BF)
    gz_ref[N + 1] = jnp.zeros((64, C), BF)
    gain = gain_ref[...]
    shift = shift_ref[...]

    def mlp(m, carry):
        rows = pl.ds(m * 8, 8)
        z = z_ref[rows].reshape(512, C)
        average = jnp.mean(z, axis=1, keepdims=True)
        centered = z - average
        variance = jnp.mean(centered * centered, axis=1, keepdims=True)
        inv_std = lax.rsqrt(variance + 1e-06)
        normed = centered * inv_std
        zn = (normed * gain + shift).astype(BF)
        og = o_ref[rows].reshape(512, C)
        hidden = dot(zn, win_ref[...])
        cdf = 0.5 * (1.0 + lax.erf(hidden * (1.0 / math.sqrt(2.0))))
        pdf = jnp.exp(-0.5 * hidden * hidden) * (1.0 / math.sqrt(2.0 * math.pi))
        act = (hidden * cdf).astype(BF)
        slope = cdf + hidden * pdf
        out = x_ref[rows].reshape(512, C).astype(F32) + dot(act, wout_ref[...])
        x_ref[rows] = out.astype(BF).reshape(8, 64, C)
        grad_hidden = (dot(og, wout_t_ref[...]) * slope).astype(BF)
        gwout_ref[...] += dot(og.T, act)
        gwin_ref[...] += dot(zn.T, grad_hidden)
        grad_normed = dot(grad_hidden, win_t_ref[...])
        gains_ref[0:8] += jnp.sum((grad_normed * normed).reshape(64, 8, C), axis=0)
        gains_ref[8:16] += jnp.sum(grad_normed.reshape(64, 8, C), axis=0)
        scaled = grad_normed * gain
        grad_z = inv_std * (
            scaled
            - jnp.mean(scaled, axis=1, keepdims=True)
            - normed * jnp.mean(scaled * normed, axis=1, keepdims=True)
        )
        grad_z = grad_z.astype(BF).reshape(8, 64, C)
        gz_ref[pl.ds(m * 8 + 1, 8)] = grad_z
        for h in range(2):
            for t in range(T):
                for u in range(2):
                    g_ref[h, rows, t * 16 : (t + 1) * 16, u * HALF : (u + 1) * HALF] = grad_z[
                        :, t * 32 + u * 16 : t * 32 + u * 16 + 16, h * HALF : (h + 1) * HALF
                    ]
        return carry

    for m in range(4):
        mlp(m, 0)

    def unorder(m, carry):
        for t in range(T):
            rows = pl.ds(m * 8, 8)
            block = x_ref[rows, t * 32 : (t + 1) * 32].reshape(256, C)
            result_ref[t, rows] = dot(merge_ref[...], block).astype(BF).reshape(8, 32, C)
        return carry

    for m in range(4):
        unorder(m, 0)
    half = wide_ref.shape[0] // 2
    wide_ref[:half, 0:256] = gwout_ref[...].T.astype(BF).reshape(half, 256, C)
    wide_ref[half:, 0:256] = gwin_ref[...].T.astype(BF).reshape(half, 256, C)
    copies = fetch(
        [
            (wide_ref.at[:, 0:256], wide_out.at[:, 0:256]),
            (result_ref, result_out),
            (gz_ref, gz_out),
        ],
        sems,
    )

    for h in range(2):
        gt_ref[h] = g_ref[h].reshape(1024, 256).T
    eye = lax.broadcasted_iota(jnp.int32, (HALF, HALF), 0) == lax.broadcasted_iota(
        jnp.int32, (HALF, HALF), 1
    )

    def taps(a, carry):
        for h in range(2):
            prod = dot(gt_ref[h], q_ref[h, pl.ds(a, 32)].reshape(1024, 1024))
            sums = [None] * 7
            for d in range(4):
                for s in range(2):
                    for u in range(2):
                        b = 2 * d + s - u
                        if 0 <= b <= 6:
                            lane = d * 256 + s * HALF
                            block = jnp.where(
                                eye, prod[u * HALF : (u + 1) * HALF, lane : lane + HALF], 0.0
                            )
                            sums[b] = block if sums[b] is None else sums[b] + block
            rows = [jnp.sum(block, axis=0, keepdims=True) for block in sums]
            rows.append(jnp.zeros((1, HALF), F32))
            small_ref[a, :, h * HALF : (h + 1) * HALF] = jnp.concatenate(rows, axis=0)
        return carry

    for a in range(7):
        taps(a, 0)
    small_ref[7] = jnp.concatenate(
        [
            jnp.sum(gains_ref[0:8], axis=0, keepdims=True),
            jnp.sum(gains_ref[8:16], axis=0, keepdims=True),
            jnp.zeros((6, C), F32),
        ],
        axis=0,
    )
    blank = jnp.zeros((8, 8, C), F32)
    wide_ref[:, 256:272] = jnp.concatenate([small_ref[...], blank], axis=1).astype(BF)
    copies += fetch([(wide_ref.at[:, 256:272], wide_out.at[:, 256:272])], sems.at[3:4])
    for copy in copies:
        copy.wait()


def rims_kernel(
    gz_ref,
    kern_ref,
    row_ref,
    gsel_ref,
    rsel_ref,
    sent_ref,
    near_ref,
    w_ref,
    g_ref,
    r_ref,
    edge_ref,
):
    build_weights(kern_ref, w_ref, True)
    for h in range(2):
        g_ref[h, 0:6] = jnp.zeros((6, 32, 1024), BF)
        g_ref[h, 12:18] = jnp.zeros((6, 32, 1024), BF)
        r_ref[0, h, 0:3] = jnp.zeros((3, 16, 1024), BF)
        r_ref[0, h, 19:22] = jnp.zeros((3, 16, 1024), BF)
        r_ref[1, h, 0:2] = jnp.zeros((2, 16, 1024), BF)
        r_ref[1, h, 19:22] = jnp.zeros((3, 16, 1024), BF)

    def rim_pairs(i, carry):
        block = gz_ref[pl.ds(2 * i, 3)].reshape(192, C)
        picked = dot(gsel_ref[512:], block).astype(BF)
        spread(picked[0:128], r_ref.at[0], 3 + i, 0)
        spread(picked[128:256], r_ref.at[1], 2 + i, 0)
        return carry

    for i in range(16):
        rim_pairs(i, 0)
    last = dot(rsel_ref[...], gz_ref[N : N + 2].reshape(128, C)).astype(BF)
    spread(last, r_ref.at[1], 18, 0)
    for first, row in ((0, 6), (1, 7), (29, 9), (30, 10)):
        picked = dot(gsel_ref[0:512], gz_ref[first : first + 3].reshape(192, C)).astype(BF)
        for v in range(2):
            for t in range(T):
                at = (v * T + t) * 128
                spread(picked[at : at + 128], g_ref, row + v, t * 16)

    for h in range(2):
        acc = None
        for a in range(7):
            k, v = a // 2, a % 2
            lhs = jnp.concatenate(
                [
                    g_ref[h, a : a + 3].reshape(96, 1024),
                    g_ref[h, 9 + a : 12 + a].reshape(96, 1024),
                    r_ref[v, h, k : k + 19].reshape(304, 1024),
                ],
                axis=0,
            )
            part = dot(lhs, w_ref[h, a])
            acc = part if acc is None else acc + part
        edge_ref[h, 0:496] = acc.astype(BF)
        edge_ref[h, 496:512] = jnp.zeros((16, 256), BF)

    edges = jnp.concatenate(
        [
            jnp.concatenate([edge_ref[0, :, 0:HALF], edge_ref[1, :, 0:HALF]], axis=1),
            jnp.concatenate([edge_ref[0, :, HALF:], edge_ref[1, :, HALF:]], axis=1),
        ],
        axis=0,
    )
    rows = SENT + LOCAL
    pick = lax.broadcasted_iota(jnp.int32, (rows, 1024), 0) == row_ref[...]
    back = dot(jnp.where(pick, 1.0, 0.0).astype(BF), edges)
    sent_ref[...] = back[:SENT].astype(BF).reshape(PARTS, KB, C)
    near_ref[...] = back[SENT:].reshape(2, 3, N, C)


def inside_kernel(h, gz_in, kern_ref, gsel_ref, inner_ref, w_ref, g_ref, gz_ref, sems):
    copies = fetch([(gz_in, gz_ref)], sems)
    build_weights(kern_ref, w_ref, True, (h,))
    g_ref[0:3] = jnp.zeros((3, 32, 1024), BF)
    g_ref[35:38] = jnp.zeros((3, 32, 1024), BF)
    copies[0].wait()

    def pairs(i, carry):
        block = gz_ref[pl.ds(2 * i, 3), :, h * HALF : (h + 1) * HALF].reshape(192, HALF)
        picked = dot(gsel_ref[0:512], block).astype(BF)
        for v in range(2):
            for t in range(T):
                for ds in range(8):
                    at = (v * T + t) * 128 + ds * 16
                    rows = slice(t * 16, (t + 1) * 16)
                    lanes = slice(ds * HALF, (ds + 1) * HALF)
                    g_ref[3 + 2 * i + v, rows, lanes] = picked[at : at + 16]
        return carry

    for i in range(16):
        pairs(i, 0)

    def inside(m, carry):
        acc = None
        for a in range(7):
            lhs = g_ref[pl.ds(m * 8 + a, 8)].reshape(256, 1024)
            part = dot(lhs, w_ref[0, a])
            acc = part if acc is None else acc + part
        acc = acc.reshape(8, T, 16, 256)
        for t in range(T):
            for u in range(2):
                inner_ref[t, pl.ds(m * 8, 8), pl.ds(u, 16, stride=2), :] = acc[
                    :, t, :, u * HALF : (u + 1) * HALF
                ]
        return carry

    lax.fori_loop(0, 4, inside, 0)


def join_kernel(sent_ref, wide_ref, out_ref):
    total = wide_ref[0].astype(F32)
    for rep in range(1, wide_ref.shape[0]):
        total = total + wide_ref[rep].astype(F32)
    total = total.astype(BF)
    out_ref[:, 0:KB] = sent_ref[...]
    out_ref[:, KB : KB + 16] = total[0:256].reshape(PARTS, 16, C)
    for part in range(PARTS):
        out_ref[part, KB + 16 :] = total[256:272]


def return_kernel(got_ref, source_ref, out_ref, small_ref):
    pick = lax.broadcasted_iota(jnp.int32, (SENT, SENT), 0) == source_ref[...]
    pick = jnp.where(pick, 1.0, 0.0).astype(BF)
    routed = dot(pick, got_ref[:, 0:KB].reshape(SENT, C)).astype(BF)
    out_ref[:, 0:KB] = routed.reshape(PARTS, KB, C)
    total = got_ref[0, KB:].astype(F32)
    for part in range(1, PARTS):
        total = total + got_ref[part, KB:].astype(F32)
    total = total.astype(BF)
    small_ref[...] = total[16:]
    for part in range(PARTS):
        out_ref[part, KB:] = total[:16]


def spread_kernel(got_ref, small_ref, out_ref):
    wide = got_ref[:, KB : KB + 16].reshape(256, C)
    small = small_ref[...]
    for rep in range(out_ref.shape[0]):
        out_ref[rep, 0:256] = wide
        out_ref[rep, 256:272] = small


def final_kernel(inner0_ref, inner1_ref, near_ref, og_ref, recv_ref, pixel_ref, out_ref):
    recv = recv_ref[:, 0:KB].reshape(SENT, C)
    for t in range(T):
        for m in range(2):
            rows = N * N // 2
            first = (t * 2 + m) * rows
            pick = lax.broadcasted_iota(jnp.int32, (rows, SENT), 0) + first == pixel_ref[...]
            back = dot(jnp.where(pick, 1.0, 0.0).astype(BF), recv).reshape(N // 2, N, C)
            half = slice(m * N // 2, (m + 1) * N // 2)
            inner = jnp.concatenate([inner0_ref[t, half], inner1_ref[t, half]], axis=2)
            total = inner + og_ref[t, half].astype(F32) + back
            if (t, m) == (1, 0):
                total = jnp.concatenate([total[:3] + near_ref[0], total[3:]], axis=0)
            if (t, m) == (0, 1):
                total = jnp.concatenate([total[:-3], total[-3:] + near_ref[1]], axis=0)
            out_ref[t, half] = total.astype(BF)


def unpack_kernel(norm_scale, got_ref, wout_ref, win_ref, taps_ref, gain_ref, shift_ref):
    half = got_ref.shape[0] // 2
    small = got_ref[:, 256:272].astype(F32) * norm_scale
    taps_ref[...] = small[0:7, 0:7]
    gain_ref[...] = small[7, 0:1]
    shift_ref[...] = small[7, 1:2]
    for rep in range(half):
        rows = slice(rep * 256, (rep + 1) * 256)
        wout_ref[rows] = got_ref[rep, 0:256].astype(F32) * norm_scale
        win_ref[:, rows] = (got_ref[half + rep, 0:256].astype(F32) * norm_scale).T


def call(kernel, outs, scratch=(), out_specs=None, in_specs=None, flops=0, vmem=16):
    options = {}
    if flops:
        options["cost_estimate"] = pl.CostEstimate(
            flops=flops, bytes_accessed=10_000_000, transcendentals=0
        )
    if in_specs is not None:
        options["in_specs"] = in_specs
    if out_specs is not None:
        options["out_specs"] = out_specs
    return pl.pallas_call(
        kernel,
        out_shape=outs,
        scratch_shapes=list(scratch),
        compiler_params=pltpu.CompilerParams(vmem_limit_bytes=vmem * MIB),
        **options,
    )


def swap(array, axes):
    return lax.all_to_all(array, axes, 0, 0, tiled=True)


def body(
    fields,
    out_grad,
    kernel,
    ln_gain,
    ln_shift,
    w_in,
    w_out,
    edge_tile,
    edge_code,
    corner_tile,
    corner_code,
):
    x = fields[0]
    og = out_grad[0]
    faces = lax.axis_size("face")
    reps = lax.axis_size("rep")
    devices = faces * reps
    norm_scale = 1.0 / math.sqrt(devices * T * N * N)
    offset = lax.axis_index("face") * T
    vm = pl.BlockSpec(memory_space=pltpu.VMEM)
    hbm = pl.BlockSpec(memory_space=pltpu.HBM)
    shape = jax.ShapeDtypeStruct

    codes = jnp.concatenate([edge_code, corner_code], axis=1) // 4
    flags = lax.dynamic_slice_in_dim(codes, offset, T, 0)
    odd = jnp.arange(edge_tile.shape[0]) % T
    blocks = []
    for block in range(3):
        edge = [edge_of(t, block) for t in range(T)]
        tile = jnp.where(odd == 0, edge_tile[:, edge[0]], edge_tile[:, edge[1]])
        code = jnp.where(odd == 0, edge_code[:, edge[0]], edge_code[:, edge[1]]) % 4
        place = jnp.where(code == 1, 16, jnp.where(code == 3, 32, 0))
        first = tile // T * KB + place + tile % T * 6
        blocks.append((first[:, None] + np.arange(6)).reshape(-1, 12))
    corners = corner_tile // T * KB + corner_tile % T * 16 + 12 + corner_code % 4
    corners = corners.reshape(-1, T, 4)
    none = jnp.full_like(corners[:, 0], -1)
    source = jnp.concatenate(
        [blocks[0], corners[:, 0], blocks[1], corners[:, 1], blocks[2], none], axis=1
    ).reshape(-1)
    pick = (source[:, None] == jnp.arange(SENT, dtype=jnp.int32)).astype(BF)
    rim_rows = rows_of(tables_of(forward_rim_pixels()), flags)
    edge_rows = rows_of(tables_of(backward_rim_pixels()), flags)
    pixels = source_pixels()

    taps = jnp.pad(kernel.astype(F32), ((0, 0), (0, 1), (0, 0)))

    sent = call(
        pack_kernel,
        shape((PARTS, KB, C), BF),
        scratch=(
            pltpu.VMEM((T, N, N, C), BF),
            pltpu.VMEM((SENT, 1), jnp.int32),
            pltpu.SemaphoreType.DMA((2,)),
        ),
        in_specs=[hbm, hbm],
        out_specs=vm,
        vmem=60,
    )(x, pixels[:, None])
    split = split_columns()
    ordered = shape((N, 64, C), BF)
    x_ord, og_ord = call(order_kernel, (ordered, ordered), flops=3_000_000_000)(
        x, og, split.astype(BF)
    )
    got = swap(sent, "face")
    routed = dot(pick, got.reshape(-1, C)).astype(BF).reshape(got.shape)
    got = swap(routed, "face")

    result, wide, gz = call(
        forward_kernel,
        (
            shape((T, N, N, C), BF),
            shape((reps, 272, C), BF),
            shape((N + 2, 64, C), BF),
        ),
        scratch=(
            pltpu.VMEM((T, N, N, C), BF),
            pltpu.VMEM((PARTS, KB, C), BF),
            pltpu.VMEM((C, HID), BF),
            pltpu.VMEM((HID, C), BF),
            pltpu.VMEM((HID, C), BF),
            pltpu.VMEM((C, HID), BF),
            pltpu.VMEM((512, 4 * (N + SIDE)), BF),
            pltpu.VMEM((256, 256), BF),
            pltpu.VMEM((T, N, N, C), BF),
            pltpu.VMEM((N + 2, 64, C), BF),
            pltpu.VMEM((reps, 272, C), BF),
            pltpu.VMEM((N + 6, T, N, C), BF),
            pltpu.VMEM((N + 6, T * SIDE, C), BF),
            pltpu.VMEM((2, N + 6, 32, 1024), BF),
            pltpu.VMEM((2, 7, 1024, 256), BF),
            pltpu.VMEM((N, 64, C), BF),
            pltpu.VMEM((N, 64, C), BF),
            pltpu.VMEM((N, 64, C), F32),
            pltpu.VMEM((C, HID), F32),
            pltpu.VMEM((C, HID), F32),
            pltpu.VMEM((16, C), F32),
            pltpu.VMEM((2, N, 32, 256), BF),
            pltpu.VMEM((2, 256, 1024), BF),
            pltpu.VMEM((8, 8, C), F32),
            pltpu.SemaphoreType.DMA((7,)),
        ),
        in_specs=[hbm] * 4 + [vm] * 4 + [hbm] * 6,
        out_specs=(hbm, hbm, hbm),
        flops=40_000_000_000,
        vmem=60,
    )(
        x,
        x_ord,
        og_ord,
        got,
        rim_rows[None],
        taps,
        ln_gain[None],
        ln_shift[None],
        w_in,
        w_out,
        w_in.T,
        w_out.T,
        pair_selector().astype(BF),
        split.T.astype(BF),
    )

    wide = swap(wide, "rep")
    gsel = grad_selector().astype(BF)
    sent, near = call(
        rims_kernel,
        (shape((PARTS, KB, C), BF), shape((2, 3, N, C), F32)),
        scratch=(
            pltpu.VMEM((2, 7, 1024, 256), BF),
            pltpu.VMEM((2, 18, 32, 1024), BF),
            pltpu.VMEM((2, 2, 22, 16, 1024), BF),
            pltpu.VMEM((2, 512, 256), BF),
        ),
        flops=12_000_000_000,
        vmem=32,
    )(gz, taps, edge_rows[None], gsel, grad_rim_selector().astype(BF))
    inner = [
        call(
            functools.partial(inside_kernel, h),
            shape((T, N, N, HALF), F32),
            scratch=(
                pltpu.VMEM((1, 7, 1024, 256), BF),
                pltpu.VMEM((N + 6, 32, 1024), BF),
                pltpu.VMEM((N + 2, 64, C), BF),
                pltpu.SemaphoreType.DMA((1,)),
            ),
            in_specs=[hbm, vm, vm],
            out_specs=vm,
            flops=9_000_000_000,
            vmem=20,
        )(gz, taps, gsel)
        for h in range(2)
    ]
    sent = call(join_kernel, shape((PARTS, KB + 32, C), BF))(sent, wide)
    got = swap(sent, "face")
    got, inner[1] = lax.optimization_barrier((got, inner[1]))
    routed, small = call(
        return_kernel, (shape((PARTS, KB + 16, C), BF), shape((16, C), BF))
    )(got, source[None])
    got = swap(routed, "face")
    wide = call(spread_kernel, shape((reps, 272, C), BF))(got, small)
    wide = swap(wide, "rep")
    grad_input = call(final_kernel, shape((T, N, N, C), BF), flops=5_000_000_000)(
        *inner, near, og, got, pixels[None]
    )
    grad_wout, grad_win, grad_taps, grad_gain, grad_shift = call(
        functools.partial(unpack_kernel, norm_scale),
        (
            shape((HID, C), F32),
            shape((C, HID), F32),
            shape(kernel.shape, F32),
            shape((1, C), F32),
            shape((1, C), F32),
        ),
    )(wide)
    return (
        result[None],
        grad_input[None],
        grad_taps,
        grad_gain[0],
        grad_shift[0],
        grad_win,
        grad_wout,
    )


def solution(mesh):
    return jax.shard_map(
        body,
        mesh=mesh,
        in_specs=(P("rep", "face"), P("rep", "face")) + (P(),) * 9,
        out_specs=(P("rep", "face"), P("rep", "face")) + (P(),) * 5,
        check_vma=False,
    )
```
